32 devices in a mesh: band: 4 (over y, x), expert: 8 (over z, core).
Axes of the slice: x: 2, y: 2, z: 4, core: 2. Of those that a mesh axis runs over, the one named last changes fastest.
Arguments:
- features: bfloat16 [8, 32, 64, 512], P('expert', None, 'band'), may hold values from -18 to 18
- routes: int32 [8, 4, 32, 16, 1], P('expert', 'band'), may hold values from 0 to 7; in each aligned block of 512 rows (0 to 511, 512 to 1023, ..., all dimensions but the last counted through in order) at most 128 rows name the same one
- qkv_regular: bfloat16 [512, 1536], replicated, may hold values from -0.25 to 0.25
- proj_regular: bfloat16 [512, 512], replicated, may hold values from -0.25 to 0.25
- table_regular: float32 [225, 16], replicated, may hold values from -4 to 4
- gain_regular: float32 [512], replicated, may hold values from 0.5 to 1.5
- mlp_up: bfloat16 [512, 2048], replicated, may hold values from -0.25 to 0.25
- mlp_down: bfloat16 [2048, 512], replicated, may hold values from -0.125 to 0.125
- gain_mlp: float32 [512], replicated, may hold values from 0.5 to 1.5
- qkv_shifted: bfloat16 [512, 1536], replicated, may hold values from -0.25 to 0.25
- proj_shifted: bfloat16 [512, 512], replicated, may hold values from -0.25 to 0.25
- table_shifted: float32 [225, 16], replicated, may hold values from -4 to 4
- gain_shifted: float32 [512], replicated, may hold values from 0.5 to 1.5
- expert_in: bfloat16 [8, 512, 2048], P('expert', None, 'band'), may hold values from -0.25 to 0.25
- expert_out: bfloat16 [8, 2048, 512], P('expert', 'band'), may hold values from -0.125 to 0.125
- gain_expert: float32 [512], replicated, may hold values from 0.5 to 1.5
Outputs:
- encoded: bfloat16 [8, 32, 64, 512], P('expert', None, 'band')
The draws below stay inside these ranges and needn't reach their ends.
Inputs may be any that keep to these rules, and one draw needn't show every extreme that they name: `routes`: within one crop and one band (an aligned block of 512 tokens) no expert is named by more than 128 tokens, a bound that some block reaches.
All inputs are finite; a program needn't handle non-finite values.
Results may differ from the reference program's by a relative error of at most 0.015.
Values may be sent and summed in bfloat16 or wider, within the bound.
No kernel may reach another device: no remote copies, remote signals or barrier semaphores. Data moves between devices by JAX's collectives and lax.ppermute only.
A program may use at most 128 MiB of HBM per device.

```python
import math
import jax
import jax.numpy as jnp
import numpy as np
from jax import lax

D = 512
HEADS = 16
FF = 2048
WIN = 8
GRID_H = 32
BAND_W = 16
BANDS = 4
GRID_W = 64
CROPS = 8
EXPERTS = 8
SEC = 512
CAP = 128
TABLE = 225


def draw_features(key, part):
    key_base = jax.random.fold_in(key, 11)
    key_noise, key_rows, key_cols = jax.random.split(key_base, 3)
    full_shape = (CROPS, GRID_H, GRID_W, D)
    noise = jnp.clip(jax.random.normal(key_noise, full_shape, jnp.float32), -3.0, 3.0)
    row_scale = jnp.exp(jax.random.uniform(key_rows, (CROPS, GRID_H, GRID_W, 1), jnp.float32, math.log(0.3), math.log(3.0)))
    col_scale = jnp.exp(jax.random.uniform(key_cols, (D,), jnp.float32, math.log(0.5), math.log(2.0)))
    return (noise * row_scale * col_scale).astype(jnp.bfloat16)


def shard_levels(key, shape, pieces, least, top_value):
    loudness, own = 1.0, jax.random.fold_in(key, 6)
    for dim, parts in pieces:
        steps = jnp.exp(jax.random.uniform(jax.random.fold_in(own, dim), (parts,), jnp.float32, least / len(pieces), top_value / len(pieces)))
        loudness = loudness * jnp.repeat(steps, shape[dim] // parts).reshape([-1 if axis == dim else 1 for axis in range(len(shape))])
    return loudness


def routed_block(own_key, own, number, rows, amount, top, most, lean):
    order = jax.random.permutation(own_key, amount)
    crowded, usual = load_shares(amount, rows * top, most, lean, True), load_shares(amount, rows * top, most, lean, False)
    places = jnp.arange(amount)

    def named(sizes, rotation):
        used = int((sizes > 0).sum())
        fixed = max(1, used // 4)
        shifted = fixed + (places - fixed + rotation * (used - fixed)) % max(1, amount - fixed)
        return jnp.zeros((amount,), jnp.int32).at[order[jnp.where(places < fixed, places, shifted)]].set(jnp.asarray(sizes, jnp.int32))

    sizes = jnp.where(number % 4 == 0, named(crowded, number // 4), named(usual, number - number // 4 - 1))
    mixed = jax.random.permutation(jax.random.fold_in(own, 3), amount)
    giver, receiver = mixed[0:amount // 2 * 2:2], mixed[1:amount // 2 * 2:2]
    slack = jnp.minimum(sizes[giver] - 1, most - sizes[receiver]) // 2
    slack = jnp.where((giver == order[0]) | (receiver == order[0]) | (sizes[receiver] == 0), 0, jnp.maximum(slack, 0))
    shifted = jax.random.randint(jax.random.fold_in(own, 4), (amount // 2,), 0, 1 << 20) % (slack + 1)
    sizes = sizes.at[giver].add(-shifted).at[receiver].add(shifted)
    items = jnp.searchsorted(jnp.cumsum(sizes), jnp.arange(rows * top), side="right").astype(jnp.int32)
    listing = items.reshape(top, rows).T
    listing = listing[jax.random.permutation(jax.random.fold_in(own, 1), rows)]
    rotation = jax.random.randint(jax.random.fold_in(own, 2), (rows, 1), 0, top)
    return jnp.take_along_axis(listing, (jnp.arange(top)[None, :] + rotation) % top, axis=1)


def load_shares(number_of, total, reach, slope, full):
    portions = [(1 << 20) // math.isqrt(standing ** slope) + 1 for standing in range(1, number_of + 1)]
    largest = reach if full else min(reach, max(-(-total // number_of), total * portions[0] // sum(portions)))
    least = 1 if total - largest >= number_of - 1 else 0
    counts, rest = [largest] + [least] * (number_of - 1), total - largest - least * (number_of - 1)
    while rest > 0:
        candidates = [i for i in range(1, number_of) if counts[i] < largest] or [i for i in range(1, number_of) if counts[i] < reach]
        whole, remaining = sum([portions[i] for i in candidates]), rest
        for i in candidates:
            more = min(reach - counts[i], max(1, remaining * portions[i] // whole), rest)
            counts[i] = counts[i] + more
            rest = rest - more
    return np.array(counts)


def gaussian(own_key, shape, width, reach, shards=(), kind=jnp.bfloat16):
    result = width * jax.random.normal(own_key, shape, jnp.float32)
    if shards:
        result = result * shard_levels(own_key, shape, shards, -0.22, 0.18)
    return jnp.clip(result, -reach, reach).astype(kind)


def setup_inputs(seed: int = 0) -> dict:
    seeds = jax.random.split(jax.random.key(seed), 17)
    features = draw_features(jax.random.fold_in(seeds[16], 71), 0)
    routes_keys = jax.random.split(jax.random.fold_in(seeds[1], 1), CROPS * BANDS * GRID_H * BAND_W // SEC)
    routes_turns = jax.random.permutation(jax.random.fold_in(seeds[1], 3), CROPS * BANDS * GRID_H * BAND_W // SEC)
    routes = jax.vmap(lambda own, number: routed_block(jax.random.fold_in(seeds[1], 2), own, number, SEC, EXPERTS, 1, CAP, 2))(routes_keys, routes_turns).reshape((CROPS, BANDS, GRID_H, BAND_W, 1))
    qkv_regular = gaussian(seeds[2], (D, 3 * D), D ** -0.5, 0.25)
    proj_regular = gaussian(seeds[3], (D, D), D ** -0.5, 0.25)
    table_regular = gaussian(seeds[4], (TABLE, HEADS), 1.0, 4.0, (), jnp.float32)
    gain_regular = jnp.clip(1.0 + 0.1 * jax.random.normal(seeds[5], (D,), jnp.float32), 0.5, 1.5)
    mlp_up = gaussian(seeds[6], (D, FF), D ** -0.5, 0.25)
    mlp_down = gaussian(seeds[7], (FF, D), FF ** -0.5, 0.125)
    gain_mlp = jnp.clip(1.0 + 0.1 * jax.random.normal(seeds[8], (D,), jnp.float32), 0.5, 1.5)
    qkv_shifted = gaussian(seeds[9], (D, 3 * D), D ** -0.5, 0.25)
    proj_shifted = gaussian(seeds[10], (D, D), D ** -0.5, 0.25)
    table_shifted = gaussian(seeds[11], (TABLE, HEADS), 1.0, 4.0, (), jnp.float32)
    gain_shifted = jnp.clip(1.0 + 0.1 * jax.random.normal(seeds[12], (D,), jnp.float32), 0.5, 1.5)
    expert_in = gaussian(seeds[13], (EXPERTS, D, FF), D ** -0.5, 0.25, ((0, 8), (2, 4)))
    expert_out = gaussian(seeds[14], (EXPERTS, FF, D), FF ** -0.5, 0.125, ((0, 8), (1, 4)))
    gain_expert = jnp.clip(1.0 + 0.1 * jax.random.normal(seeds[15], (D,), jnp.float32), 0.5, 1.5)
    return dict(features=features, routes=routes, qkv_regular=qkv_regular, proj_regular=proj_regular, table_regular=table_regular, gain_regular=gain_regular, mlp_up=mlp_up, mlp_down=mlp_down, gain_mlp=gain_mlp, qkv_shifted=qkv_shifted, proj_shifted=proj_shifted, table_shifted=table_shifted, gain_shifted=gain_shifted, expert_in=expert_in, expert_out=expert_out, gain_expert=gain_expert)


def layer_norm(values, gain_vec):
    centre = lax.optimization_barrier(jnp.mean(values, axis=-1, keepdims=True))
    offsets = values - centre
    spread = lax.optimization_barrier(jnp.mean(offsets * offsets, axis=-1, keepdims=True))
    return offsets * lax.rsqrt(spread + 1e-05) * gain_vec

def band_labels(places, length_cells, window):
    half_win = window // 2
    return jnp.where(places < length_cells - window, 0, jnp.where(places < length_cells - half_win, 1, 2)).astype(jnp.int32)

def partition(grid_vals, window):
    height, width_cells = grid_vals.shape[:2]
    trailing = grid_vals.shape[2:]
    split_up = grid_vals.reshape((height // window, window, width_cells // window, window) + trailing)
    order = (0, 2, 1, 3) + tuple(range(4, 4 + len(trailing)))
    return split_up.transpose(order).reshape((-1, window * window) + trailing)

def merge_windows(window_vals, height, width_cells, window):
    model_width = window_vals.shape[-1]
    split_up = window_vals.reshape(height // window, width_cells // window, window, window, model_width)
    return split_up.transpose(0, 2, 1, 3, 4).reshape(height, width_cells, model_width)

def attend(grid_in, qkv_weight, table, label_grid):
    height, width_cells, model_width = grid_in.shape
    window = WIN
    head_count = HEADS
    head_dim = model_width // head_count
    cell_count = window * window
    span_cells = 2 * window - 1
    cell_ids = jnp.arange(cell_count, dtype=jnp.int32)
    cell_row = cell_ids // window
    cell_col = cell_ids % window
    index_grid = (cell_row[:, None] - cell_row[None, :] + window - 1) * span_cells + (cell_col[:, None] - cell_col[None, :] + window - 1)
    bias_heads = jnp.take(table, index_grid.reshape(-1), axis=0).reshape(cell_count, cell_count, head_count).transpose(2, 0, 1)
    qkv_all = jnp.dot(grid_in.reshape(-1, model_width), qkv_weight, preferred_element_type=jnp.float32).astype(jnp.bfloat16)
    parted = partition(qkv_all.reshape(height, width_cells, 3 * model_width), window)
    queries = parted[:, :, :model_width].reshape(-1, cell_count, head_count, head_dim).astype(jnp.float32)
    key_rows = parted[:, :, model_width:2 * model_width].reshape(-1, cell_count, head_count, head_dim).astype(jnp.float32)
    value_rows = parted[:, :, 2 * model_width:].reshape(-1, cell_count, head_count, head_dim).astype(jnp.float32)
    label_cells = partition(label_grid, window)
    mask_add = jnp.where(label_cells[:, :, None] == label_cells[:, None, :], 0.0, -100.0).astype(jnp.float32)
    scores = jnp.einsum('wqhd,wkhd->whqk', queries, key_rows) * head_dim ** (-0.5) + bias_heads[None] + mask_add[:, None]
    weights = jnp.exp(scores - lax.optimization_barrier(jnp.max(scores, axis=-1, keepdims=True)))
    weights = (weights / lax.optimization_barrier(jnp.sum(weights, axis=-1, keepdims=True))).astype(jnp.bfloat16)
    mixed_heads = jnp.einsum('whqk,wkhd->wqhd', weights.astype(jnp.float32), value_rows).astype(jnp.bfloat16)
    return merge_windows(mixed_heads.reshape(-1, cell_count, model_width), height, width_cells, window)

def crop_blocks(grid_in, qkv_regular, proj_regular, table_regular, gain_regular, mlp_up, mlp_down, gain_mlp, qkv_shifted, proj_shifted, table_shifted, gain_shifted):
    height, width_cells, model_width = grid_in.shape
    half_win = WIN // 2
    zero_labels = jnp.zeros((height, width_cells), jnp.int32)
    heads_regular = attend(grid_in, qkv_regular, table_regular, zero_labels)
    flat_in = grid_in.reshape(-1, model_width).astype(jnp.float32)
    projected = jnp.dot(heads_regular.reshape(-1, model_width), proj_regular, preferred_element_type=jnp.float32)
    first_out = (flat_in + layer_norm(projected, gain_regular)).astype(jnp.bfloat16)
    hidden_mlp = jax.nn.gelu(jnp.dot(first_out, mlp_up, preferred_element_type=jnp.float32), approximate=False).astype(jnp.bfloat16)
    dense_out = jnp.dot(hidden_mlp, mlp_down, preferred_element_type=jnp.float32)
    second_out = (first_out.astype(jnp.float32) + layer_norm(dense_out, gain_mlp)).astype(jnp.bfloat16)
    rolled = jnp.roll(second_out.reshape(height, width_cells, model_width), (-half_win, -half_win), axis=(0, 1))
    row_places = jnp.arange(height, dtype=jnp.int32)
    col_places = jnp.arange(width_cells, dtype=jnp.int32)
    label_grid = band_labels(row_places, height, WIN)[:, None] * 3 + band_labels(col_places, width_cells, WIN)[None, :]
    heads_shifted = jnp.roll(attend(rolled, qkv_shifted, table_shifted, label_grid), (half_win, half_win), axis=(0, 1))
    projected_two = jnp.dot(heads_shifted.reshape(-1, model_width), proj_shifted, preferred_element_type=jnp.float32)
    third_out = (second_out.astype(jnp.float32) + layer_norm(projected_two, gain_shifted)).astype(jnp.bfloat16)
    return third_out.reshape(height, width_cells, model_width)

def reference(features, routes, qkv_regular, proj_regular, table_regular, gain_regular, mlp_up, mlp_down, gain_mlp, qkv_shifted, proj_shifted, table_shifted, gain_shifted, expert_in, expert_out, gain_expert):

    def crop_step(grid_in):
        return crop_blocks(grid_in, qkv_regular, proj_regular, table_regular, gain_regular, mlp_up, mlp_down, gain_mlp, qkv_shifted, proj_shifted, table_shifted, gain_shifted)
    streams = lax.map(crop_step, features)
    section_count = CROPS * BANDS
    sections = streams.reshape(CROPS, GRID_H, BANDS, BAND_W, D).transpose(0, 2, 1, 3, 4).reshape(section_count, SEC, D)
    route_rows = routes.reshape(section_count, SEC).astype(jnp.int32)
    onehot = (route_rows[:, :, None] == jnp.arange(EXPERTS, dtype=jnp.int32)[None, None, :]).astype(jnp.int32)
    positions = lax.optimization_barrier(jnp.sum(jnp.cumsum(onehot, axis=1) * onehot, axis=2)) - 1
    section_ids = jnp.arange(section_count, dtype=jnp.int32)[:, None]
    target = ((route_rows * section_count + section_ids) * CAP + positions).reshape(-1).astype(jnp.int32)
    buffer_rows = jnp.zeros((EXPERTS * section_count * CAP, D), jnp.bfloat16).at[target].set(sections.reshape(-1, D))

    def one_expert(packed):
        rows_in, weight_in, weight_out = packed
        hidden = jax.nn.gelu(jnp.dot(rows_in, weight_in, preferred_element_type=jnp.float32), approximate=False).astype(jnp.bfloat16)
        return jnp.dot(hidden, weight_out, preferred_element_type=jnp.float32).astype(jnp.bfloat16)
    mapped = lax.map(one_expert, (buffer_rows.reshape(EXPERTS, section_count * CAP, D), expert_in, expert_out))
    expert_rows = mapped.reshape(-1, D)[target]
    encoded = (sections.reshape(-1, D).astype(jnp.float32) + layer_norm(expert_rows.astype(jnp.float32), gain_expert)).astype(jnp.bfloat16)
    return encoded.reshape(CROPS, BANDS, GRID_H, BAND_W, D).transpose(0, 2, 1, 3, 4).reshape(CROPS, GRID_H, GRID_W, D)
```

```python
import functools
import math

import jax
import jax.numpy as jnp
from jax import lax
from jax.experimental import pallas as pl
from jax.experimental.pallas import tpu as pltpu
from jax.sharding import PartitionSpec as P

HEADS = 16
WIN = 8
HALF = WIN // 2
SPAN = 2 * WIN - 1
LANES = 128
LOG2E = math.log2(math.e)
CLOSED = -1e30
MASKED = -100.0 * LOG2E
BF = jnp.bfloat16
F32 = jnp.float32
I32 = jnp.int32

NN = (((1,), (0,)), ((), ()))
NT = (((1,), (1,)), ((), ()))


def dot(a, b, dims=NN):
    return lax.dot_general(a, b, dims, preferred_element_type=F32)


def iota(shape, dim):
    return lax.broadcasted_iota(I32, shape, dim)


def gelu(x):
    return 0.5 * x * (1.0 + lax.erf(x * math.sqrt(0.5)))


def layer_norm(values, gain):
    centre = jnp.mean(values, axis=-1, keepdims=True)
    offsets = values - centre
    spread = jnp.mean(offsets * offsets, axis=-1, keepdims=True)
    return offsets * lax.rsqrt(spread + 1e-05) * gain


def pick(row, idx):
    low = jnp.broadcast_to(row[:, :LANES], idx.shape)
    high = jnp.broadcast_to(row[:, LANES:], idx.shape)
    from_low = jnp.take_along_axis(
        low, jnp.minimum(idx, LANES - 1), axis=1, mode="promise_in_bounds"
    )
    from_high = jnp.take_along_axis(
        high, jnp.maximum(idx - LANES, 0), axis=1, mode="promise_in_bounds"
    )
    return jnp.where(idx < LANES, from_low, from_high)


def offset_index(row_p, col_p, row_q, col_q):
    return (row_p - row_q + WIN - 1) * SPAN + (col_p - col_q + WIN - 1)


def own_bias(tab_ref, first_head, bias_ref, band_width, shift):
    strip = WIN * band_width
    p, q = iota((strip, strip), 0), iota((strip, strip), 1)
    row_p, col_p = lax.div(p, band_width), lax.rem(p, band_width) + shift
    row_q, col_q = lax.div(q, band_width), lax.rem(q, band_width) + shift
    idx = offset_index(row_p, lax.rem(col_p, WIN), row_q, lax.rem(col_q, WIN))
    same = lax.div(col_p, WIN) == lax.div(col_q, WIN)
    for h in range(HEADS):
        row = tab_ref[first_head + h : first_head + h + 1, :]
        tile, part = divmod(h, 4)
        bias_ref[tile, :, part * strip : (part + 1) * strip] = jnp.where(
            same, pick(row, idx), CLOSED
        )


def halo_places(band_width):
    strip, halo = WIN * band_width, 2 * WIN * HALF
    p, q = iota((strip, 2 * halo), 0), iota((strip, 2 * halo), 1)
    row_p, col_p = lax.div(p, band_width), lax.rem(p, band_width) + HALF
    key = lax.rem(q, halo)
    right = key >= WIN * HALF
    cell = lax.rem(key, WIN * HALF)
    row_q = lax.div(cell, HALF)
    col_q = lax.rem(cell, HALF) + jnp.where(right, band_width + HALF, 0)
    return row_p, col_p, row_q, col_q, right, q < halo


def halo_bias(tab_ref, first_head, bias_ref, band_width, at_first, at_last):
    row_p, col_p, row_q, col_q, right, front = halo_places(band_width)
    idx = offset_index(row_p, lax.rem(col_p, WIN), row_q, lax.rem(col_q, WIN))
    same = lax.div(col_p, WIN) == lax.div(col_q, WIN)
    edge = jnp.where(right, at_last, at_first) > 0
    wide = front.shape[1]
    for pair in range(HEADS // 2):
        h = first_head + 2 * pair
        value = jnp.where(
            front, pick(tab_ref[h : h + 1, :], idx), pick(tab_ref[h + 1 : h + 2, :], idx)
        )
        value = jnp.where(same, value + jnp.where(edge, MASKED, 0.0), CLOSED)
        tile, part = divmod(pair, 2)
        bias_ref[tile, :, part * wide : (part + 1) * wide] = value


def head_masks(parts):
    lane_head = lax.div(iota((1, LANES), 1), LANES // parts)
    return [jnp.where(lane_head == h, 1.0, 0.0).astype(BF) for h in range(parts)]


def sum_columns(keys, parts):
    shape = (parts * keys, LANES)
    return jnp.where(
        lax.div(iota(shape, 0), keys) == lax.div(iota(shape, 1), LANES // parts), 1.0, 0.0
    ).astype(BF)


def by_head(block, masks):
    return jnp.concatenate([block * mask for mask in masks], axis=0)


def front_kernel(
    band_width,
    x_ref,
    wqkv_ref,
    wproj_ref,
    tab_ref,
    gain_ref,
    up_ref,
    down_ref,
    gain_mlp_ref,
    out_ref,
    left_ref,
    right_ref,
    qkv,
    bias,
    heads,
    second,
):
    rows, width = x_ref.shape
    strip = WIN * band_width
    head_dim = width // HEADS
    parts = LANES // head_dim
    x = x_ref[...]
    for part in range(3):
        cols = slice(part * width, (part + 1) * width)
        product = dot(x, wqkv_ref[:, cols])
        if part == 0:
            product = product * (LOG2E * head_dim**-0.5)
        qkv[:, cols] = product.astype(BF)
    own_bias(tab_ref, 0, bias, band_width, 0)
    masks = head_masks(parts)
    ones = sum_columns(strip, parts)

    def tile_step(t, carry):
        lanes = pl.ds(pl.multiple_of(t * LANES, LANES), LANES)
        lanes_k = pl.ds(pl.multiple_of(width + t * LANES, LANES), LANES)
        lanes_v = pl.ds(pl.multiple_of(2 * width + t * LANES, LANES), LANES)
        bias_tile = bias.at[t]
        for g in range(rows // strip):
            tokens = slice(g * strip, (g + 1) * strip)
            keys = by_head(qkv[tokens, lanes_k], masks)
            scores = dot(qkv[tokens, lanes], keys, NT) + bias_tile[...]
            probs = []
            for h in range(parts):
                s = scores[:, h * strip : (h + 1) * strip]
                probs.append(jnp.exp2(s - jnp.max(s, axis=-1, keepdims=True)).astype(BF))
            values = jnp.concatenate([by_head(qkv[tokens, lanes_v], masks), ones], axis=1)
            both = dot(jnp.concatenate(probs, axis=1), values)
            heads[tokens, lanes] = (both[:, :LANES] / both[:, LANES:]).astype(BF)
        return carry

    lax.fori_loop(0, width // LANES, tile_step, 0)

    half = rows // 2
    hidden = up_ref.shape[1]
    for r in range(2):
        tokens = slice(r * half, (r + 1) * half)
        projected = dot(heads[tokens, :], wproj_ref[...])
        first = (x_ref[tokens, :].astype(F32) + layer_norm(projected, gain_ref[...])).astype(BF)
        total = jnp.zeros((half, width), F32)
        for f in range(hidden // width):
            cols = slice(f * width, (f + 1) * width)
            act = gelu(dot(first, up_ref[:, cols])).astype(BF)
            total = total + dot(act, down_ref[cols, :])
        second[tokens, :] = (first.astype(F32) + layer_norm(total, gain_mlp_ref[...])).astype(BF)
    turn = HALF * band_width
    rolled = jnp.concatenate([second[turn:, :], second[:turn, :]], axis=0)
    out_ref[...] = rolled
    sent = left_ref.shape[0]
    r, t = iota((sent, rows), 0), iota((sent, rows), 1)
    place = lax.div(r, HALF) * band_width + lax.rem(r, HALF)
    left_ref[...] = dot(jnp.where(t == place, 1.0, 0.0).astype(BF), rolled).astype(BF)
    place = place + (band_width - HALF)
    right_ref[...] = dot(jnp.where(t == place, 1.0, 0.0).astype(BF), rolled).astype(BF)


def middle_kernel(
    band_width,
    experts,
    capacity,
    info_ref,
    x_ref,
    wqkv_ref,
    tab_ref,
    routes_ref,
    qkv_ref,
    bias_ref,
    bias_halo_ref,
    slot_row_ref,
    slot_col_ref,
):
    rows, width = x_ref.shape
    head_dim = width // HEADS
    x = x_ref[...]
    for part in range(3):
        cols = slice(part * width, (part + 1) * width)
        product = dot(x, wqkv_ref[:, cols])
        if part == 0:
            product = product * (LOG2E * head_dim**-0.5)
        qkv_ref[:, cols] = product.astype(BF)
    own_bias(tab_ref, HEADS, bias_ref, band_width, HALF)
    halo_bias(tab_ref, HEADS, bias_halo_ref, band_width, info_ref[0], info_ref[1])
    routes = routes_ref[...]
    named = jnp.where(iota((experts, rows), 0) == routes, 1.0, 0.0)
    a, b = iota((rows, rows), 0), iota((rows, rows), 1)
    upto = jnp.where(a <= b, 1.0, 0.0).astype(BF)
    count = dot(named.astype(BF), upto)
    base = iota((experts, rows), 0).astype(F32) * capacity - 1.0
    slot = jnp.sum(named * (count + base), axis=0, keepdims=True)
    slot_row_ref[...] = jnp.broadcast_to(slot, slot_row_ref.shape).astype(I32)
    same = jnp.where(a == b, 1.0, 0.0).astype(BF)
    named_col = dot(same, named.astype(BF), NT)
    before = jnp.where(a >= b, 1.0, 0.0).astype(BF)
    count_col = dot(before, named_col.astype(BF))
    base_col = iota((rows, experts), 1).astype(F32) * capacity - 1.0
    slot_col = jnp.sum(named_col * (count_col + base_col), axis=1, keepdims=True)
    slot_col_ref[...] = jnp.broadcast_to(slot_col, slot_col_ref.shape).astype(I32)


def shifted_kernel(
    band_width,
    capacity,
    info_ref,
    qkv_ref,
    x_ref,
    from_left_ref,
    from_right_ref,
    wqkv_ref,
    bias_ref,
    bias_halo_ref,
    wproj_ref,
    gain_ref,
    slot_row_ref,
    *rest,
):
    third_ref, *out_refs, halo_kv, heads = rest
    rows, width = x_ref.shape
    strip = WIN * band_width
    side = WIN * HALF
    halo = 2 * side
    groups = rows // strip
    head_dim = width // HEADS
    parts = LANES // head_dim
    arrived = jnp.concatenate(
        [
            ref[g * side : (g + 1) * side, :]
            for g in range(groups)
            for ref in (from_left_ref, from_right_ref)
        ],
        axis=0,
    )
    halo_kv[...] = dot(arrived, wqkv_ref[:, width:]).astype(BF)
    masks = head_masks(parts)
    ones = jnp.concatenate([sum_columns(strip, parts), sum_columns(halo, parts)], axis=0)
    p, q = iota((strip, strip), 0), iota((strip, strip), 1)
    turned = HALF * band_width
    apart = jnp.where((p < turned) != (q < turned), MASKED, 0.0)
    row_p, _, row_q, _, right, front = halo_places(band_width)
    edge = jnp.where(right, info_ref[1], info_ref[0]) > 0
    crossed = (row_p < HALF) != (row_q < HALF)
    apart_halo = jnp.where(jnp.logical_and(crossed, jnp.logical_not(edge)), MASKED, 0.0)
    wide = 2 * halo

    def tile_step(t, carry):
        lanes = pl.ds(pl.multiple_of(t * LANES, LANES), LANES)
        lanes_k = pl.ds(pl.multiple_of(width + t * LANES, LANES), LANES)
        lanes_v = pl.ds(pl.multiple_of(2 * width + t * LANES, LANES), LANES)
        bias_tile = bias_ref.at[t]
        bias_halo_tile = bias_halo_ref.at[t]
        for g in range(groups):
            tokens = slice(g * strip, (g + 1) * strip)
            outside = slice(g * halo, (g + 1) * halo)
            queries = qkv_ref[tokens, lanes]
            scores = dot(queries, by_head(qkv_ref[tokens, lanes_k], masks), NT)
            scores = scores + bias_tile[...]
            scores_halo = dot(queries, by_head(halo_kv[outside, lanes], masks), NT)
            scores_halo = scores_halo + bias_halo_tile[...]
            probs, probs_halo = [], []
            for pair in range(parts // 2):
                s_halo = scores_halo[:, pair * wide : (pair + 1) * wide]
                if g == groups - 1:
                    s_halo = s_halo + apart_halo
                tops = []
                for k in range(2):
                    h = 2 * pair + k
                    s = scores[:, h * strip : (h + 1) * strip]
                    if g == groups - 1:
                        s = s + apart
                    mine = front if k == 0 else jnp.logical_not(front)
                    top = jnp.max(
                        jnp.maximum(s, jnp.where(mine, s_halo, CLOSED)), axis=-1, keepdims=True
                    )
                    tops.append(top)
                    probs.append(jnp.exp2(s - top).astype(BF))
                probs_halo.append(
                    jnp.exp2(s_halo - jnp.where(front, tops[0], tops[1])).astype(BF)
                )
            values = jnp.concatenate(
                [by_head(qkv_ref[tokens, lanes_v], masks), by_head(halo_kv[outside, lanes_k], masks)],
                axis=0,
            )
            both = dot(
                jnp.concatenate(probs + probs_halo, axis=1),
                jnp.concatenate([values, ones], axis=1),
            )
            heads[tokens, lanes] = (both[:, :LANES] / both[:, LANES:]).astype(BF)
        return carry

    lax.fori_loop(0, width // LANES, tile_step, 0)
    projected = dot(heads[...], wproj_ref[...])
    third = (x_ref[...].astype(F32) + layer_norm(projected, gain_ref[...])).astype(BF)
    third_ref[...] = third
    slot = slot_row_ref[0:1, :]
    for s, ref in enumerate(out_refs):
        places = iota((capacity, rows), 0) + s * capacity
        ref[...] = dot(jnp.where(places == slot, 1.0, 0.0).astype(BF), third).astype(BF)


def expert_kernel(amount, quarters, *refs):
    x_refs, rest = refs[:amount], refs[amount:]
    in_refs, rest = rest[:quarters], rest[quarters:]
    out_w_refs, out_refs = rest[:quarters], rest[quarters:]
    x = jnp.concatenate([ref[...] for ref in x_refs], axis=0)
    total = jnp.zeros(x.shape, F32)
    for w_in, w_out in zip(in_refs, out_w_refs):
        total = total + dot(gelu(dot(x, w_in[...])).astype(BF), w_out[...])
    each = x_refs[0].shape[0]
    for k, ref in enumerate(out_refs):
        ref[...] = total[k * each : (k + 1) * each, :].astype(BF)


def final_kernel(band_width, capacity, third_ref, slot_col_ref, gain_ref, *rest):
    *result_refs, out_ref = rest
    rows, width = third_ref.shape
    results = jnp.concatenate([ref[...] for ref in result_refs], axis=0)
    slot = slot_col_ref[...]
    chosen = jnp.concatenate(
        [
            jnp.where(slot == iota(slot.shape, 1) + k * LANES, 1.0, 0.0).astype(BF)
            for k in range(results.shape[0] // LANES)
        ],
        axis=1,
    )
    picked = dot(chosen, results)
    encoded = (third_ref[...].astype(F32) + layer_norm(picked, gain_ref[...])).astype(BF)
    turn = HALF * band_width
    out_ref[turn:, :] = encoded[: rows - turn, :]
    out_ref[:turn, :] = encoded[rows - turn :, :]


def call(kernel, outs, ins, scratch=(), scalars=0, limit=32, flops=0):
    vmem = pl.BlockSpec(memory_space=pltpu.VMEM)
    smem = pl.BlockSpec(memory_space=pltpu.SMEM)
    size = sum(math.prod(a.shape) * a.dtype.itemsize for a in list(ins) + list(outs))
    return pl.pallas_call(
        kernel,
        out_shape=outs,
        in_specs=[smem] * scalars + [vmem] * (len(ins) - scalars),
        out_specs=[vmem] * len(outs),
        scratch_shapes=list(scratch),
        compiler_params=pltpu.CompilerParams(vmem_limit_bytes=limit << 20),
        cost_estimate=pl.CostEstimate(flops=flops, bytes_accessed=size, transcendentals=0),
    )(*ins)


def shape_of(*dims, dtype=BF):
    return jax.ShapeDtypeStruct(dims, dtype)


def swap(block, axis, bits):
    return lax.ppermute(block, axis, [(i, i ^ bits) for i in range(lax.axis_size(axis))])


def gather_blocks(block, axis, steps):
    blocks = {0: block}
    for bit in steps:
        blocks.update({at ^ bit: swap(held, axis, bit) for at, held in list(blocks.items())})
    return [blocks[at] for at in range(len(blocks))]


def local(
    features,
    routes,
    qkv_regular,
    proj_regular,
    table_regular,
    gain_regular,
    mlp_up,
    mlp_down,
    gain_mlp,
    qkv_shifted,
    proj_shifted,
    table_shifted,
    gain_shifted,
    expert_in,
    expert_out,
    gain_expert,
):
    crop_count, height, band_width, width = features.shape
    rows = height * band_width
    band_count = lax.axis_size("band")
    band_index = lax.axis_index("band")
    experts = lax.axis_size("expert")
    capacity = 2 * rows // experts
    hidden = mlp_up.shape[1]
    strip = WIN * band_width
    tiles = width // LANES
    wide = LANES // (width // HEADS) * strip
    wide_halo = LANES // (width // HEADS) * 2 * WIN * HALF
    sent = height * HALF

    steps = [1 << k for k in range(band_count.bit_length() - 1)]
    weights_in = gather_blocks(expert_in[0], "band", steps)
    weights_out = gather_blocks(expert_out[0], "band", steps[::-1])

    tables = jnp.concatenate([table_regular, table_shifted], axis=1).T * LOG2E
    tables = jnp.pad(tables, ((0, 0), (0, 2 * LANES - tables.shape[1])))
    info = jnp.stack([band_index == 0, band_index == band_count - 1]).astype(I32)
    turn = HALF * band_width
    route_row = jnp.roll(routes.reshape(1, rows), -turn, axis=1) ^ lax.axis_index("expert")

    second, to_left, to_right = call(
        functools.partial(front_kernel, band_width),
        [shape_of(rows, width), shape_of(sent, width), shape_of(sent, width)],
        [
            features.reshape(rows, width),
            qkv_regular,
            proj_regular,
            tables,
            gain_regular.reshape(1, width),
            mlp_up,
            mlp_down,
            gain_mlp.reshape(1, width),
        ],
        [
            pltpu.VMEM((rows, 3 * width), BF),
            pltpu.VMEM((tiles, strip, wide), F32),
            pltpu.VMEM((rows, width), BF),
            pltpu.VMEM((rows, width), BF),
        ],
        flops=2 * rows * width * (4 * width + 2 * hidden),
    )
    ring = range(band_count)
    from_right = lax.ppermute(to_left, "band", [(i, (i - 1) % band_count) for i in ring])
    from_left = lax.ppermute(to_right, "band", [(i, (i + 1) % band_count) for i in ring])
    qkv, bias, bias_halo, slot_row, slot_col = call(
        functools.partial(middle_kernel, band_width, experts, capacity),
        [
            shape_of(rows, 3 * width),
            shape_of(tiles, strip, wide, dtype=F32),
            shape_of(tiles, strip, wide_halo, dtype=F32),
            shape_of(8, rows, dtype=I32),
            shape_of(rows, LANES, dtype=I32),
        ],
        [info, second, qkv_shifted, tables, route_row],
        scalars=1,
        flops=2 * rows * width * 3 * width,
    )
    third, *outgoing = call(
        functools.partial(shifted_kernel, band_width, capacity),
        [shape_of(rows, width)] + [shape_of(capacity, width)] * experts,
        [
            info,
            qkv,
            second,
            from_left,
            from_right,
            qkv_shifted,
            bias,
            bias_halo,
            proj_shifted,
            gain_shifted.reshape(1, width),
            slot_row,
        ],
        [
            pltpu.VMEM((2 * sent, 2 * width), BF),
            pltpu.VMEM((rows, width), BF),
        ],
        scalars=1,
        flops=2 * rows * width * 4 * width,
    )
    arrived = [outgoing[0]] + [swap(outgoing[s], "expert", s) for s in range(1, experts)]
    amount = experts // 4
    results = []
    for k in range(0, experts, amount):
        results += call(
            functools.partial(expert_kernel, amount, band_count),
            [shape_of(capacity, width)] * amount,
            arrived[k : k + amount] + weights_in + weights_out,
            flops=4 * amount * capacity * width * hidden,
        )
    returned = [results[0]] + [swap(results[s], "expert", s) for s in range(1, experts)]
    encoded = call(
        functools.partial(final_kernel, band_width, capacity),
        [shape_of(rows, width)],
        [third, slot_col, gain_expert.reshape(1, width)] + returned,
        flops=2 * rows * width * 2 * rows,
    )[0]
    return encoded.reshape(crop_count, height, band_width, width)


def solution(mesh):
    return jax.shard_map(
        local,
        mesh=mesh,
        in_specs=(
            P("expert", None, "band", None),
            P("expert", "band", None, None, None),
        )
        + (P(),) * 11
        + (
            P("expert", None, "band"),
            P("expert", "band", None),
            P(),
        ),
        out_specs=P("expert", None, "band", None),
        check_vma=False,
    )
```

```python
import functools
import math

import jax
import jax.numpy as jnp
from jax import lax
from jax.experimental import pallas as pl
from jax.experimental.pallas import tpu as pltpu
from jax.sharding import PartitionSpec as P

HEADS = 16
WIN = 8
HALF = WIN // 2
SPAN = 2 * WIN - 1
LANES = 128
LOG2E = math.log2(math.e)
CLOSED = -1e30
MASKED = -100.0 * LOG2E
BF = jnp.bfloat16
F32 = jnp.float32
I32 = jnp.int32

NN = (((1,), (0,)), ((), ()))
NT = (((1,), (1,)), ((), ()))


def dot(a, b, dims=NN):
    return lax.dot_general(a, b, dims, preferred_element_type=F32)


def iota(shape, dim):
    return lax.broadcasted_iota(I32, shape, dim)


def gelu(x):
    return 0.5 * x * (1.0 + lax.erf(x * math.sqrt(0.5)))


def layer_norm(values, gain):
    centre = jnp.mean(values, axis=-1, keepdims=True)
    offsets = values - centre
    spread = jnp.mean(offsets * offsets, axis=-1, keepdims=True)
    return offsets * lax.rsqrt(spread + 1e-05) * gain


def pick(row, idx):
    low = jnp.broadcast_to(row[:, :LANES], idx.shape)
    high = jnp.broadcast_to(row[:, LANES:], idx.shape)
    from_low = jnp.take_along_axis(
        low, jnp.minimum(idx, LANES - 1), axis=1, mode="promise_in_bounds"
    )
    from_high = jnp.take_along_axis(
        high, jnp.maximum(idx - LANES, 0), axis=1, mode="promise_in_bounds"
    )
    return jnp.where(idx < LANES, from_low, from_high)


def head_rows(table_ref, tab_ref):
    tab_ref[:, : table_ref.shape[1]] = table_ref[...] * LOG2E


def offset_index(row_p, col_p, row_q, col_q):
    return (row_p - row_q + WIN - 1) * SPAN + (col_p - col_q + WIN - 1)


def own_bias(tab_ref, bias_ref, band_width, shift):
    strip = WIN * band_width
    p, q = iota((strip, strip), 0), iota((strip, strip), 1)
    row_p, col_p = lax.div(p, band_width), lax.rem(p, band_width) + shift
    row_q, col_q = lax.div(q, band_width), lax.rem(q, band_width) + shift
    idx = offset_index(row_p, lax.rem(col_p, WIN), row_q, lax.rem(col_q, WIN))
    same = lax.div(col_p, WIN) == lax.div(col_q, WIN)
    for h in range(HEADS):
        row = tab_ref[h : h + 1, :]
        tile, part = divmod(h, 4)
        bias_ref[tile, :, part * strip : (part + 1) * strip] = jnp.where(
            same, pick(row, idx), CLOSED
        )


def halo_places(band_width):
    strip, halo = WIN * band_width, 2 * WIN * HALF
    p, q = iota((strip, 2 * halo), 0), iota((strip, 2 * halo), 1)
    row_p, col_p = lax.div(p, band_width), lax.rem(p, band_width) + HALF
    key = lax.rem(q, halo)
    right = key >= WIN * HALF
    cell = lax.rem(key, WIN * HALF)
    row_q = lax.div(cell, HALF)
    col_q = lax.rem(cell, HALF) + jnp.where(right, band_width + HALF, 0)
    return row_p, col_p, row_q, col_q, right, q < halo


def halo_bias(tab_ref, bias_ref, band_width, at_first, at_last):
    row_p, col_p, row_q, col_q, right, front = halo_places(band_width)
    idx = offset_index(row_p, lax.rem(col_p, WIN), row_q, lax.rem(col_q, WIN))
    same = lax.div(col_p, WIN) == lax.div(col_q, WIN)
    edge = jnp.where(right, at_last, at_first) > 0
    wide = front.shape[1]
    for pair in range(HEADS // 2):
        h = 2 * pair
        value = jnp.where(
            front, pick(tab_ref[h : h + 1, :], idx), pick(tab_ref[h + 1 : h + 2, :], idx)
        )
        value = jnp.where(same, value + jnp.where(edge, MASKED, 0.0), CLOSED)
        tile, part = divmod(pair, 2)
        bias_ref[tile, :, part * wide : (part + 1) * wide] = value


def head_masks(parts):
    lane_head = lax.div(iota((1, LANES), 1), LANES // parts)
    return [jnp.where(lane_head == h, 1.0, 0.0).astype(BF) for h in range(parts)]


def sum_columns(keys, parts):
    shape = (parts * keys, LANES)
    return jnp.where(
        lax.div(iota(shape, 0), keys) == lax.div(iota(shape, 1), LANES // parts), 1.0, 0.0
    ).astype(BF)


def by_head(block, masks):
    return jnp.concatenate([block * mask for mask in masks], axis=0)


def fetch(sems, *pairs):
    copies = [pltpu.make_async_copy(a, b, sems.at[i]) for i, (a, b) in enumerate(pairs)]
    for copy in copies:
        copy.start()
    return copies


def front_kernel(
    band_width,
    table_hbm,
    x_hbm,
    wqkv_hbm,
    wproj_hbm,
    gain_hbm,
    up_hbm,
    down_hbm,
    gain_mlp_hbm,
    out_ref,
    left_ref,
    right_ref,
    x_ref,
    wqkv_ref,
    wproj_ref,
    gain_ref,
    up_ref,
    down_ref,
    gain_mlp_ref,
    table_ref,
    sems,
    tab_ref,
    qkv,
    bias,
    heads,
    act,
    second,
):
    rows, width = x_ref.shape
    strip = WIN * band_width
    head_dim = width // HEADS
    parts = LANES // head_dim
    copies = fetch(
        sems,
        (table_hbm, table_ref),
        (x_hbm, x_ref),
        (wqkv_hbm, wqkv_ref),
    )
    copies[0].wait()
    head_rows(table_ref, tab_ref)
    own_bias(tab_ref, bias, band_width, 0)
    copies[1].wait()
    copies[2].wait()
    copies = fetch(
        sems.at[3:],
        (wproj_hbm, wproj_ref),
        (gain_hbm, gain_ref),
        (up_hbm, up_ref),
        (down_hbm, down_ref),
        (gain_mlp_hbm, gain_mlp_ref),
    )
    x = x_ref[...]
    for part in range(3):
        cols = slice(part * width, (part + 1) * width)
        product = dot(x, wqkv_ref[:, cols])
        if part == 0:
            product = product * (LOG2E * head_dim**-0.5)
        qkv[:, cols] = product.astype(BF)
    masks = head_masks(parts)
    ones = sum_columns(strip, parts)

    def tile_step(t, carry):
        lanes = pl.ds(pl.multiple_of(t * LANES, LANES), LANES)
        lanes_k = pl.ds(pl.multiple_of(width + t * LANES, LANES), LANES)
        lanes_v = pl.ds(pl.multiple_of(2 * width + t * LANES, LANES), LANES)
        bias_tile = bias.at[t]
        for g in range(rows // strip):
            tokens = slice(g * strip, (g + 1) * strip)
            keys = by_head(qkv[tokens, lanes_k], masks)
            scores = dot(qkv[tokens, lanes], keys, NT) + bias_tile[...]
            probs = []
            for h in range(parts):
                s = scores[:, h * strip : (h + 1) * strip]
                probs.append(jnp.exp2(s - jnp.max(s, axis=-1, keepdims=True)).astype(BF))
            values = jnp.concatenate([by_head(qkv[tokens, lanes_v], masks), ones], axis=1)
            both = dot(jnp.concatenate(probs, axis=1), values)
            heads[tokens, lanes] = (both[:, :LANES] / both[:, LANES:]).astype(BF)
        return carry

    lax.fori_loop(0, width // LANES, tile_step, 0)
    for copy in copies:
        copy.wait()
    projected = dot(heads[...], wproj_ref[...])
    first = (x_ref[...].astype(F32) + layer_norm(projected, gain_ref[...])).astype(BF)
    act[...] = gelu(dot(first, up_ref[...])).astype(BF)
    dense = layer_norm(dot(act[...], down_ref[...]), gain_mlp_ref[...])
    second[...] = (first.astype(F32) + dense).astype(BF)
    turn = HALF * band_width
    rolled = jnp.concatenate([second[turn:, :], second[:turn, :]], axis=0)
    out_ref[...] = rolled
    sent = left_ref.shape[0]
    r, t = iota((sent, rows), 0), iota((sent, rows), 1)
    place = lax.div(r, HALF) * band_width + lax.rem(r, HALF)
    left_ref[...] = dot(jnp.where(t == place, 1.0, 0.0).astype(BF), rolled).astype(BF)
    place = place + (band_width - HALF)
    right_ref[...] = dot(jnp.where(t == place, 1.0, 0.0).astype(BF), rolled).astype(BF)


def middle_kernel(
    band_width,
    experts,
    capacity,
    info_ref,
    x_ref,
    routes_ref,
    table_hbm,
    wqkv_hbm,
    in_hbm,
    in_next,
    out_hbm,
    out_next,
    qkv_ref,
    bias_ref,
    bias_halo_ref,
    slot_row_ref,
    slot_col_ref,
    wqkv_ref,
    in_pair,
    out_pair,
    table_ref,
    sems,
    tab_ref,
):
    rows, width = x_ref.shape
    head_dim = width // HEADS
    copies = fetch(
        sems,
        (table_hbm, table_ref),
        (wqkv_hbm, wqkv_ref),
        (in_hbm, in_pair.at[0]),
        (in_next, in_pair.at[1]),
        (out_hbm, out_pair.at[0]),
        (out_next, out_pair.at[1]),
    )
    copies[0].wait()
    head_rows(table_ref, tab_ref)
    own_bias(tab_ref, bias_ref, band_width, HALF)
    halo_bias(tab_ref, bias_halo_ref, band_width, info_ref[0], info_ref[1])
    routes = routes_ref[...]
    named = jnp.where(iota((experts, rows), 0) == routes, 1.0, 0.0)
    a, b = iota((rows, rows), 0), iota((rows, rows), 1)
    upto = jnp.where(a <= b, 1.0, 0.0).astype(BF)
    count = dot(named.astype(BF), upto)
    base = iota((experts, rows), 0).astype(F32) * capacity - 1.0
    slot = jnp.sum(named * (count + base), axis=0, keepdims=True)
    slot_row_ref[...] = jnp.broadcast_to(slot, slot_row_ref.shape).astype(I32)
    same = jnp.where(a == b, 1.0, 0.0).astype(BF)
    named_col = dot(same, named.astype(BF), NT)
    before = jnp.where(a >= b, 1.0, 0.0).astype(BF)
    count_col = dot(before, named_col.astype(BF))
    base_col = iota((rows, experts), 1).astype(F32) * capacity - 1.0
    slot_col = jnp.sum(named_col * (count_col + base_col), axis=1, keepdims=True)
    slot_col_ref[...] = jnp.broadcast_to(slot_col, slot_col_ref.shape).astype(I32)
    copies[1].wait()
    x = x_ref[...]
    for part in range(3):
        cols = slice(part * width, (part + 1) * width)
        product = dot(x, wqkv_ref[:, cols])
        if part == 0:
            product = product * (LOG2E * head_dim**-0.5)
        qkv_ref[:, cols] = product.astype(BF)
    for copy in copies[2:]:
        copy.wait()


def shifted_kernel(
    band_width,
    capacity,
    info_ref,
    qkv_ref,
    x_ref,
    from_left_ref,
    from_right_ref,
    wqkv_ref,
    bias_ref,
    bias_halo_ref,
    slot_row_ref,
    wproj_hbm,
    gain_hbm,
    *rest,
):
    third_ref, *out_refs, halo_kv, heads, wproj_ref, gain_ref, sems = rest
    copies = fetch(sems, (wproj_hbm, wproj_ref), (gain_hbm, gain_ref))
    rows, width = x_ref.shape
    strip = WIN * band_width
    side = WIN * HALF
    halo = 2 * side
    groups = rows // strip
    head_dim = width // HEADS
    parts = LANES // head_dim
    arrived = jnp.concatenate(
        [
            ref[g * side : (g + 1) * side, :]
            for g in range(groups)
            for ref in (from_left_ref, from_right_ref)
        ],
        axis=0,
    )
    halo_kv[...] = dot(arrived, wqkv_ref[:, width:]).astype(BF)
    masks = head_masks(parts)
    ones = jnp.concatenate([sum_columns(strip, parts), sum_columns(halo, parts)], axis=0)
    p, q = iota((strip, strip), 0), iota((strip, strip), 1)
    turned = HALF * band_width
    apart = jnp.where((p < turned) != (q < turned), MASKED, 0.0)
    row_p, _, row_q, _, right, front = halo_places(band_width)
    edge = jnp.where(right, info_ref[1], info_ref[0]) > 0
    crossed = (row_p < HALF) != (row_q < HALF)
    apart_halo = jnp.where(jnp.logical_and(crossed, jnp.logical_not(edge)), MASKED, 0.0)
    wide = 2 * halo

    def tile_step(t, carry):
        lanes = pl.ds(pl.multiple_of(t * LANES, LANES), LANES)
        lanes_k = pl.ds(pl.multiple_of(width + t * LANES, LANES), LANES)
        lanes_v = pl.ds(pl.multiple_of(2 * width + t * LANES, LANES), LANES)
        bias_tile = bias_ref.at[t]
        bias_halo_tile = bias_halo_ref.at[t]
        for g in range(groups):
            tokens = slice(g * strip, (g + 1) * strip)
            outside = slice(g * halo, (g + 1) * halo)
            queries = qkv_ref[tokens, lanes]
            scores = dot(queries, by_head(qkv_ref[tokens, lanes_k], masks), NT)
            scores = scores + bias_tile[...]
            scores_halo = dot(queries, by_head(halo_kv[outside, lanes], masks), NT)
            scores_halo = scores_halo + bias_halo_tile[...]
            probs, probs_halo = [], []
            for pair in range(parts // 2):
                s_halo = scores_halo[:, pair * wide : (pair + 1) * wide]
                if g == groups - 1:
                    s_halo = s_halo + apart_halo
                tops = []
                for k in range(2):
                    h = 2 * pair + k
                    s = scores[:, h * strip : (h + 1) * strip]
                    if g == groups - 1:
                        s = s + apart
                    mine = front if k == 0 else jnp.logical_not(front)
                    top = jnp.max(
                        jnp.maximum(s, jnp.where(mine, s_halo, CLOSED)), axis=-1, keepdims=True
                    )
                    tops.append(top)
                    probs.append(jnp.exp2(s - top).astype(BF))
                probs_halo.append(
                    jnp.exp2(s_halo - jnp.where(front, tops[0], tops[1])).astype(BF)
                )
            values = jnp.concatenate(
                [by_head(qkv_ref[tokens, lanes_v], masks), by_head(halo_kv[outside, lanes_k], masks)],
                axis=0,
            )
            both = dot(
                jnp.concatenate(probs + probs_halo, axis=1),
                jnp.concatenate([values, ones], axis=1),
            )
            heads[tokens, lanes] = (both[:, :LANES] / both[:, LANES:]).astype(BF)
        return carry

    lax.fori_loop(0, width // LANES, tile_step, 0)
    for copy in copies:
        copy.wait()
    projected = dot(heads[...], wproj_ref[...])
    third = (x_ref[...].astype(F32) + layer_norm(projected, gain_ref[...])).astype(BF)
    third_ref[...] = third
    slot = slot_row_ref[0:1, :]
    for s, ref in enumerate(out_refs):
        places = iota((capacity, rows), 0) + s * capacity
        ref[...] = dot(jnp.where(places == slot, 1.0, 0.0).astype(BF), third).astype(BF)


def expert_kernel(amount, *refs):
    x_refs, (in_own, in_far, out_own, out_far), out_refs = (
        refs[:amount],
        refs[amount : amount + 4],
        refs[amount + 4 :],
    )
    in_refs = (in_own.at[0], in_own.at[1], in_far.at[0], in_far.at[1])
    out_w_refs = (out_own.at[0], out_far.at[0], out_own.at[1], out_far.at[1])
    x = jnp.concatenate([ref[...] for ref in x_refs], axis=0)
    total = jnp.zeros(x.shape, F32)
    for w_in, w_out in zip(in_refs, out_w_refs):
        total = total + dot(gelu(dot(x, w_in[...])).astype(BF), w_out[...])
    each = x_refs[0].shape[0]
    for k, ref in enumerate(out_refs):
        ref[...] = total[k * each : (k + 1) * each, :].astype(BF)


def final_kernel(band_width, capacity, third_ref, slot_col_ref, gain_hbm, *rest):
    *result_refs, out_ref, gain_ref, sems = rest
    copies = fetch(sems, (gain_hbm, gain_ref))
    rows, width = third_ref.shape
    results = jnp.concatenate([ref[...] for ref in result_refs], axis=0)
    slot = slot_col_ref[...]
    chosen = jnp.concatenate(
        [
            jnp.where(slot == iota(slot.shape, 1) + k * LANES, 1.0, 0.0).astype(BF)
            for k in range(results.shape[0] // LANES)
        ],
        axis=1,
    )
    picked = dot(chosen, results)
    copies[0].wait()
    encoded = (third_ref[...].astype(F32) + layer_norm(picked, gain_ref[...])).astype(BF)
    turn = HALF * band_width
    out_ref[turn:, :] = encoded[: rows - turn, :]
    out_ref[:turn, :] = encoded[rows - turn :, :]


def call(kernel, outs, ins, places, scratch=(), limit=32, flops=0, size=None):
    spaces = {"s": pltpu.SMEM, "v": pltpu.VMEM, "h": pltpu.HBM, "a": pl.ANY}
    if size is None:
        size = sum(math.prod(a.shape) * a.dtype.itemsize for a in list(ins) + list(outs))
    results = pl.pallas_call(
        kernel,
        out_shape=outs,
        in_specs=[pl.BlockSpec(memory_space=spaces[p]) for p in places],
        out_specs=[pl.BlockSpec(memory_space=pltpu.VMEM)] * len(outs),
        scratch_shapes=list(scratch),
        compiler_params=pltpu.CompilerParams(vmem_limit_bytes=limit << 20),
        cost_estimate=pl.CostEstimate(flops=flops, bytes_accessed=size, transcendentals=0),
    )(*ins)
    return list(results)


def shape_of(*dims, dtype=BF):
    return jax.ShapeDtypeStruct(dims, dtype)


def swap(block, axis, bits):
    return lax.ppermute(block, axis, [(i, i ^ bits) for i in range(lax.axis_size(axis))])


def local(
    features,
    routes,
    qkv_regular,
    proj_regular,
    table_regular,
    gain_regular,
    mlp_up,
    mlp_down,
    gain_mlp,
    qkv_shifted,
    proj_shifted,
    table_shifted,
    gain_shifted,
    expert_in,
    expert_out,
    gain_expert,
):
    crop_count, height, band_width, width = features.shape
    rows = height * band_width
    band_count = lax.axis_size("band")
    band_index = lax.axis_index("band")
    experts = lax.axis_size("expert")
    capacity = 2 * rows // experts
    hidden = mlp_up.shape[1]
    strip = WIN * band_width
    tiles = width // LANES
    wide = LANES // (width // HEADS) * strip
    wide_halo = LANES // (width // HEADS) * 2 * WIN * HALF
    sent = height * HALF

    in_next = swap(expert_in[0], "band", 1)
    out_next = swap(expert_out[0], "band", 2)

    info = jnp.stack([band_index == 0, band_index == band_count - 1]).astype(I32)
    turn = HALF * band_width
    route_row = jnp.roll(routes.reshape(1, rows), -turn, axis=1) ^ lax.axis_index("expert")

    second, to_left, to_right = call(
        functools.partial(front_kernel, band_width),
        [shape_of(rows, width), shape_of(sent, width), shape_of(sent, width)],
        [
            table_regular.T,
            features.reshape(rows, width),
            qkv_regular,
            proj_regular,
            gain_regular.reshape(1, width),
            mlp_up,
            mlp_down,
            gain_mlp.reshape(1, width),
        ],
        "hhhhhhhh",
        [
            pltpu.VMEM((rows, width), BF),
            pltpu.VMEM((width, 3 * width), BF),
            pltpu.VMEM((width, width), BF),
            pltpu.VMEM((1, width), F32),
            pltpu.VMEM((width, hidden), BF),
            pltpu.VMEM((hidden, width), BF),
            pltpu.VMEM((1, width), F32),
            pltpu.VMEM(table_regular.shape[::-1], F32),
            pltpu.SemaphoreType.DMA((8,)),
            pltpu.VMEM((HEADS, 2 * LANES), F32),
            pltpu.VMEM((rows, 3 * width), BF),
            pltpu.VMEM((tiles, strip, wide), F32),
            pltpu.VMEM((rows, width), BF),
            pltpu.VMEM((rows, hidden), BF),
            pltpu.VMEM((rows, width), BF),
        ],
        limit=60,
        flops=2 * rows * width * (4 * width + 2 * hidden),
    )
    ring = range(band_count)
    from_right = lax.ppermute(to_left, "band", [(i, (i - 1) % band_count) for i in ring])
    from_left = lax.ppermute(to_right, "band", [(i, (i + 1) % band_count) for i in ring])
    qkv, bias, bias_halo, slot_row, slot_col, wqkv, in_own, out_own = call(
        functools.partial(middle_kernel, band_width, experts, capacity),
        [
            shape_of(rows, 3 * width),
            shape_of(tiles, strip, wide, dtype=F32),
            shape_of(tiles, strip, wide_halo, dtype=F32),
            shape_of(8, rows, dtype=I32),
            shape_of(rows, LANES, dtype=I32),
            shape_of(width, 3 * width),
            shape_of(2, *expert_in.shape[1:]),
            shape_of(2, *expert_out.shape[1:]),
        ],
        [
            info,
            second,
            route_row,
            table_shifted.T,
            qkv_shifted,
            expert_in[0],
            in_next,
            expert_out[0],
            out_next,
        ],
        "svvhhhaha",
        [
            pltpu.VMEM(table_shifted.shape[::-1], F32),
            pltpu.SemaphoreType.DMA((6,)),
            pltpu.VMEM((HEADS, 2 * LANES), F32),
        ],
        flops=2 * rows * width * 3 * width,
    )
    from_left, from_right, in_own, out_own = lax.optimization_barrier(
        (from_left, from_right, in_own, out_own)
    )
    in_far = swap(in_own, "band", 2)
    out_far = swap(out_own, "band", 1)
    third, *outgoing = call(
        functools.partial(shifted_kernel, band_width, capacity),
        [shape_of(rows, width)] + [shape_of(capacity, width)] * experts,
        [
            info,
            qkv,
            second,
            from_left,
            from_right,
            wqkv,
            bias,
            bias_halo,
            slot_row,
            proj_shifted,
            gain_shifted.reshape(1, width),
        ],
        "svvvvvvvvhh",
        [
            pltpu.VMEM((2 * sent, 2 * width), BF),
            pltpu.VMEM((rows, width), BF),
            pltpu.VMEM((width, width), BF),
            pltpu.VMEM((1, width), F32),
            pltpu.SemaphoreType.DMA((2,)),
        ],
        flops=2 * rows * width * 4 * width,
    )
    weights = [in_own, in_far, out_own, out_far]

    def send(blocks, first):
        return [swap(block, "expert", first + k) for k, block in enumerate(blocks)]

    def compute(blocks):
        return call(
            functools.partial(expert_kernel, len(blocks)),
            [shape_of(capacity, width)] * len(blocks),
            blocks + weights,
            "v" * (len(blocks) + 4),
            flops=4 * len(blocks) * capacity * width * hidden,
        )

    far, most = experts // 2, 3 * experts // 4
    third_part = send(outgoing[far:most], far)
    *third_part, = lax.optimization_barrier((*third_part, *outgoing[most:]))
    fourth_part = send(third_part[most - far :], most)
    third_part = compute(third_part[: most - far])
    *third_part, = lax.optimization_barrier((*third_part, *outgoing[:far]))
    near = third_part[most - far :]
    near = near[:1] + send(near[1:], 1)
    back_third = send(third_part[: most - far], far)
    back_fourth = send(compute(fourth_part), most)
    half = far // 2
    first_part, second_part = compute(near[:half]), compute(near[half:])
    returned = (
        first_part[:1]
        + send(first_part[1:], 1)
        + send(second_part, half)
        + back_third
        + back_fourth
    )
    encoded = call(
        functools.partial(final_kernel, band_width, capacity),
        [shape_of(rows, width)],
        [third, slot_col, gain_expert.reshape(1, width)] + returned,
        "vvh" + "v" * experts,
        [pltpu.VMEM((1, width), F32), pltpu.SemaphoreType.DMA((1,))],
        flops=2 * rows * width * 2 * rows,
    )[0]
    return encoded.reshape(crop_count, height, band_width, width)


def solution(mesh):
    return jax.shard_map(
        local,
        mesh=mesh,
        in_specs=(
            P("expert", None, "band", None),
            P("expert", "band", None, None, None),
        )
        + (P(),) * 11
        + (
            P("expert", None, "band"),
            P("expert", "band", None),
            P(),
        ),
        out_specs=P("expert", None, "band", None),
        check_vma=False,
    )
```

```python
import functools
import math

import jax
import jax.numpy as jnp
from jax import lax
from jax.experimental import pallas as pl
from jax.experimental.pallas import tpu as pltpu
from jax.sharding import PartitionSpec as P

HEADS = 16
WIN = 8
HALF = WIN // 2
SPAN = 2 * WIN - 1
LANES = 128
LOG2E = math.log2(math.e)
CLOSED = -1e30
MASKED = -100.0 * LOG2E
BF = jnp.bfloat16
F32 = jnp.float32
I32 = jnp.int32

NN = (((1,), (0,)), ((), ()))
NT = (((1,), (1,)), ((), ()))


def dot(a, b, dims=NN):
    return lax.dot_general(a, b, dims, preferred_element_type=F32)


def iota(shape, dim):
    return lax.broadcasted_iota(I32, shape, dim)


def gelu(x):
    return 0.5 * x * (1.0 + lax.erf(x * math.sqrt(0.5)))


def layer_norm(values, gain):
    centre = jnp.mean(values, axis=-1, keepdims=True)
    offsets = values - centre
    spread = jnp.mean(offsets * offsets, axis=-1, keepdims=True)
    return offsets * lax.rsqrt(spread + 1e-05) * gain


def pick(row, idx):
    low = jnp.broadcast_to(row[:, :LANES], idx.shape)
    high = jnp.broadcast_to(row[:, LANES:], idx.shape)
    from_low = jnp.take_along_axis(
        low, jnp.minimum(idx, LANES - 1), axis=1, mode="promise_in_bounds"
    )
    from_high = jnp.take_along_axis(
        high, jnp.maximum(idx - LANES, 0), axis=1, mode="promise_in_bounds"
    )
    return jnp.where(idx < LANES, from_low, from_high)


def head_rows(table_ref, tab_ref):
    tab_ref[:, : table_ref.shape[1]] = table_ref[...] * LOG2E


def offset_index(row_p, col_p, row_q, col_q):
    return (row_p - row_q + WIN - 1) * SPAN + (col_p - col_q + WIN - 1)


def own_bias(tab_ref, bias_ref, band_width, shift):
    strip = WIN * band_width
    p, q = iota((strip, strip), 0), iota((strip, strip), 1)
    row_p, col_p = lax.div(p, band_width), lax.rem(p, band_width) + shift
    row_q, col_q = lax.div(q, band_width), lax.rem(q, band_width) + shift
    idx = offset_index(row_p, lax.rem(col_p, WIN), row_q, lax.rem(col_q, WIN))
    same = lax.div(col_p, WIN) == lax.div(col_q, WIN)
    for h in range(HEADS):
        row = tab_ref[h : h + 1, :]
        tile, part = divmod(h, 4)
        bias_ref[tile, :, part * strip : (part + 1) * strip] = jnp.where(
            same, pick(row, idx), CLOSED
        )


def halo_places(band_width):
    strip, halo = WIN * band_width, 2 * WIN * HALF
    p, q = iota((strip, 2 * halo), 0), iota((strip, 2 * halo), 1)
    row_p, col_p = lax.div(p, band_width), lax.rem(p, band_width) + HALF
    key = lax.rem(q, halo)
    right = key >= WIN * HALF
    cell = lax.rem(key, WIN * HALF)
    row_q = lax.div(cell, HALF)
    col_q = lax.rem(cell, HALF) + jnp.where(right, band_width + HALF, 0)
    return row_p, col_p, row_q, col_q, right, q < halo


def halo_bias(tab_ref, bias_ref, band_width, at_first, at_last):
    row_p, col_p, row_q, col_q, right, front = halo_places(band_width)
    idx = offset_index(row_p, lax.rem(col_p, WIN), row_q, lax.rem(col_q, WIN))
    same = lax.div(col_p, WIN) == lax.div(col_q, WIN)
    edge = jnp.where(right, at_last, at_first) > 0
    wide = front.shape[1]
    for pair in range(HEADS // 2):
        h = 2 * pair
        value = jnp.where(
            front, pick(tab_ref[h : h + 1, :], idx), pick(tab_ref[h + 1 : h + 2, :], idx)
        )
        value = jnp.where(same, value + jnp.where(edge, MASKED, 0.0), CLOSED)
        tile, part = divmod(pair, 2)
        bias_ref[tile, :, part * wide : (part + 1) * wide] = value


def head_masks(parts):
    lane_head = lax.div(iota((1, LANES), 1), LANES // parts)
    return [jnp.where(lane_head == h, 1.0, 0.0).astype(BF) for h in range(parts)]


def sum_columns(keys, parts):
    shape = (parts * keys, LANES)
    return jnp.where(
        lax.div(iota(shape, 0), keys) == lax.div(iota(shape, 1), LANES // parts), 1.0, 0.0
    ).astype(BF)


def by_head(block, masks):
    return jnp.concatenate([block * mask for mask in masks], axis=0)


def fetch(sems, *pairs):
    copies = [pltpu.make_async_copy(a, b, sems.at[i]) for i, (a, b) in enumerate(pairs)]
    for copy in copies:
        copy.start()
    return copies


def front_kernel(
    band_width,
    table_hbm,
    x_hbm,
    wqkv_hbm,
    wproj_hbm,
    gain_hbm,
    up_hbm,
    down_hbm,
    gain_mlp_hbm,
    out_ref,
    left_ref,
    right_ref,
    x_ref,
    wqkv_ref,
    wproj_ref,
    gain_ref,
    up_ref,
    down_ref,
    gain_mlp_ref,
    table_ref,
    sems,
    tab_ref,
    qkv,
    bias,
    heads,
    act,
    second,
):
    rows, width = x_ref.shape
    strip = WIN * band_width
    head_dim = width // HEADS
    parts = LANES // head_dim
    copies = fetch(
        sems,
        (table_hbm, table_ref),
        (x_hbm, x_ref),
        (wqkv_hbm, wqkv_ref),
    )
    copies[0].wait()
    head_rows(table_ref, tab_ref)
    own_bias(tab_ref, bias, band_width, 0)
    copies[1].wait()
    copies[2].wait()
    copies = fetch(
        sems.at[3:],
        (wproj_hbm, wproj_ref),
        (gain_hbm, gain_ref),
        (up_hbm, up_ref),
        (down_hbm, down_ref),
        (gain_mlp_hbm, gain_mlp_ref),
    )
    x = x_ref[...]
    for part in range(3):
        cols = slice(part * width, (part + 1) * width)
        product = dot(x, wqkv_ref[:, cols])
        if part == 0:
            product = product * (LOG2E * head_dim**-0.5)
        qkv[:, cols] = product.astype(BF)
    masks = head_masks(parts)
    ones = sum_columns(strip, parts)

    def tile_step(t, carry):
        lanes = pl.ds(pl.multiple_of(t * LANES, LANES), LANES)
        lanes_k = pl.ds(pl.multiple_of(width + t * LANES, LANES), LANES)
        lanes_v = pl.ds(pl.multiple_of(2 * width + t * LANES, LANES), LANES)
        bias_tile = bias.at[t]
        for g in range(rows // strip):
            tokens = slice(g * strip, (g + 1) * strip)
            keys = by_head(qkv[tokens, lanes_k], masks)
            scores = dot(qkv[tokens, lanes], keys, NT) + bias_tile[...]
            probs = []
            for h in range(parts):
                s = scores[:, h * strip : (h + 1) * strip]
                probs.append(jnp.exp2(s - jnp.max(s, axis=-1, keepdims=True)).astype(BF))
            values = jnp.concatenate([by_head(qkv[tokens, lanes_v], masks), ones], axis=1)
            both = dot(jnp.concatenate(probs, axis=1), values)
            heads[tokens, lanes] = (both[:, :LANES] / both[:, LANES:]).astype(BF)
        return carry

    lax.fori_loop(0, width // LANES, tile_step, 0, unroll=True)
    for copy in copies:
        copy.wait()
    projected = dot(heads[...], wproj_ref[...])
    first = (x_ref[...].astype(F32) + layer_norm(projected, gain_ref[...])).astype(BF)
    act[...] = gelu(dot(first, up_ref[...])).astype(BF)
    dense = layer_norm(dot(act[...], down_ref[...]), gain_mlp_ref[...])
    second[...] = (first.astype(F32) + dense).astype(BF)
    turn = HALF * band_width
    rolled = jnp.concatenate([second[turn:, :], second[:turn, :]], axis=0)
    out_ref[...] = rolled
    sent = left_ref.shape[0]
    r, t = iota((sent, rows), 0), iota((sent, rows), 1)
    place = lax.div(r, HALF) * band_width + lax.rem(r, HALF)
    left_ref[...] = dot(jnp.where(t == place, 1.0, 0.0).astype(BF), rolled).astype(BF)
    place = place + (band_width - HALF)
    right_ref[...] = dot(jnp.where(t == place, 1.0, 0.0).astype(BF), rolled).astype(BF)


def column_kernel(slot_row_ref, slot_col_ref):
    rows = slot_row_ref.shape[1]
    slot = slot_row_ref[...]
    digit = iota(slot.shape, 0)
    parts = jnp.where(
        digit == 0, lax.rem(slot, LANES), jnp.where(digit == 1, lax.div(slot, LANES), 0)
    )
    same = jnp.where(iota((rows, rows), 0) == iota((rows, rows), 1), 1.0, 0.0).astype(BF)
    turned = dot(same, parts.astype(F32).astype(BF), NT)
    column = turned[:, 0:1] + turned[:, 1:2] * LANES
    slot_col_ref[...] = jnp.broadcast_to(column, slot_col_ref.shape).astype(I32)


def middle_kernel(
    band_width,
    experts,
    capacity,
    info_ref,
    x_any,
    routes_ref,
    table_hbm,
    wqkv_hbm,
    in_hbm,
    in_next,
    out_hbm,
    out_next,
    qkv_ref,
    bias_ref,
    bias_halo_ref,
    slot_row_ref,
    wqkv_ref,
    in_pair,
    out_pair,
    table_ref,
    x_ref,
    sems,
    tab_ref,
):
    rows, width = x_ref.shape
    head_dim = width // HEADS
    copies = fetch(
        sems,
        (table_hbm, table_ref),
        (wqkv_hbm, wqkv_ref),
        (x_any, x_ref),
    )
    copies[0].wait()
    head_rows(table_ref, tab_ref)
    own_bias(tab_ref, bias_ref, band_width, HALF)
    halo_bias(tab_ref, bias_halo_ref, band_width, info_ref[0], info_ref[1])
    routes = routes_ref[...]
    named = jnp.where(iota((experts, rows), 0) == routes, 1.0, 0.0)
    a, b = iota((rows, rows), 0), iota((rows, rows), 1)
    upto = jnp.where(a <= b, 1.0, 0.0).astype(BF)
    count = dot(named.astype(BF), upto)
    base = iota((experts, rows), 0).astype(F32) * capacity - 1.0
    slot = jnp.sum(named * (count + base), axis=0, keepdims=True)
    slot_row_ref[...] = jnp.broadcast_to(slot, slot_row_ref.shape).astype(I32)
    copies[1].wait()
    copies[2].wait()
    copies = fetch(
        sems.at[3:],
        (in_hbm, in_pair.at[0]),
        (in_next, in_pair.at[1]),
        (out_hbm, out_pair.at[0]),
        (out_next, out_pair.at[1]),
    )
    x = x_ref[...]
    for part in range(3):
        cols = slice(part * width, (part + 1) * width)
        product = dot(x, wqkv_ref[:, cols])
        if part == 0:
            product = product * (LOG2E * head_dim**-0.5)
        qkv_ref[:, cols] = product.astype(BF)
    for copy in copies:
        copy.wait()


def shifted_kernel(
    band_width,
    capacity,
    info_ref,
    qkv_ref,
    x_ref,
    from_left_ref,
    from_right_ref,
    wqkv_ref,
    bias_ref,
    bias_halo_ref,
    slot_row_ref,
    wproj_hbm,
    gain_hbm,
    *rest,
):
    third_ref, *out_refs, halo_kv, heads, wproj_ref, gain_ref, sems = rest
    copies = fetch(sems, (wproj_hbm, wproj_ref), (gain_hbm, gain_ref))
    rows, width = x_ref.shape
    strip = WIN * band_width
    side = WIN * HALF
    halo = 2 * side
    groups = rows // strip
    head_dim = width // HEADS
    parts = LANES // head_dim
    arrived = jnp.concatenate(
        [
            ref[g * side : (g + 1) * side, :]
            for g in range(groups)
            for ref in (from_left_ref, from_right_ref)
        ],
        axis=0,
    )
    halo_kv[...] = dot(arrived, wqkv_ref[:, width:]).astype(BF)
    masks = head_masks(parts)
    ones = jnp.concatenate([sum_columns(strip, parts), sum_columns(halo, parts)], axis=0)
    p, q = iota((strip, strip), 0), iota((strip, strip), 1)
    turned = HALF * band_width
    apart = jnp.where((p < turned) != (q < turned), MASKED, 0.0)
    row_p, _, row_q, _, right, front = halo_places(band_width)
    edge = jnp.where(right, info_ref[1], info_ref[0]) > 0
    crossed = (row_p < HALF) != (row_q < HALF)
    apart_halo = jnp.where(jnp.logical_and(crossed, jnp.logical_not(edge)), MASKED, 0.0)
    wide = 2 * halo

    def tile_step(t, carry):
        lanes = pl.ds(pl.multiple_of(t * LANES, LANES), LANES)
        lanes_k = pl.ds(pl.multiple_of(width + t * LANES, LANES), LANES)
        lanes_v = pl.ds(pl.multiple_of(2 * width + t * LANES, LANES), LANES)
        bias_tile = bias_ref.at[t]
        bias_halo_tile = bias_halo_ref.at[t]
        for g in range(groups):
            tokens = slice(g * strip, (g + 1) * strip)
            outside = slice(g * halo, (g + 1) * halo)
            queries = qkv_ref[tokens, lanes]
            scores = dot(queries, by_head(qkv_ref[tokens, lanes_k], masks), NT)
            scores = scores + bias_tile[...]
            scores_halo = dot(queries, by_head(halo_kv[outside, lanes], masks), NT)
            scores_halo = scores_halo + bias_halo_tile[...]
            probs, probs_halo = [], []
            for pair in range(parts // 2):
                s_halo = scores_halo[:, pair * wide : (pair + 1) * wide]
                if g == groups - 1:
                    s_halo = s_halo + apart_halo
                tops = []
                for k in range(2):
                    h = 2 * pair + k
                    s = scores[:, h * strip : (h + 1) * strip]
                    if g == groups - 1:
                        s = s + apart
                    mine = front if k == 0 else jnp.logical_not(front)
                    top = jnp.max(
                        jnp.maximum(s, jnp.where(mine, s_halo, CLOSED)), axis=-1, keepdims=True
                    )
                    tops.append(top)
                    probs.append(jnp.exp2(s - top).astype(BF))
                probs_halo.append(
                    jnp.exp2(s_halo - jnp.where(front, tops[0], tops[1])).astype(BF)
                )
            values = jnp.concatenate(
                [by_head(qkv_ref[tokens, lanes_v], masks), by_head(halo_kv[outside, lanes_k], masks)],
                axis=0,
            )
            both = dot(
                jnp.concatenate(probs + probs_halo, axis=1),
                jnp.concatenate([values, ones], axis=1),
            )
            heads[tokens, lanes] = (both[:, :LANES] / both[:, LANES:]).astype(BF)
        return carry

    lax.fori_loop(0, width // LANES, tile_step, 0, unroll=True)
    for copy in copies:
        copy.wait()
    projected = dot(heads[...], wproj_ref[...])
    third = (x_ref[...].astype(F32) + layer_norm(projected, gain_ref[...])).astype(BF)
    third_ref[...] = third
    slot = slot_row_ref[0:1, :]
    group = max(1, 2 * LANES // capacity)
    for s in range(0, len(out_refs), group):
        places = iota((group * capacity, rows), 0) + s * capacity
        sent = dot(jnp.where(places == slot, 1.0, 0.0).astype(BF), third).astype(BF)
        for k in range(group):
            out_refs[s + k][...] = sent[k * capacity : (k + 1) * capacity, :]


def expert_kernel(amount, *refs):
    x_refs, (in_own, in_far, out_own, out_far), out_refs = (
        refs[:amount],
        refs[amount : amount + 4],
        refs[amount + 4 :],
    )
    in_refs = (in_own.at[0], in_own.at[1], in_far.at[0], in_far.at[1])
    out_w_refs = (out_own.at[0], out_far.at[0], out_own.at[1], out_far.at[1])
    x = jnp.concatenate([ref[...] for ref in x_refs], axis=0)
    total = jnp.zeros(x.shape, F32)
    for w_in, w_out in zip(in_refs, out_w_refs):
        total = total + dot(gelu(dot(x, w_in[...])).astype(BF), w_out[...])
    each = x_refs[0].shape[0]
    for k, ref in enumerate(out_refs):
        ref[...] = total[k * each : (k + 1) * each, :].astype(BF)


def final_kernel(band_width, capacity, third_ref, slot_col_ref, gain_hbm, *rest):
    *result_refs, out_ref, gain_ref, sems = rest
    copies = fetch(sems, (gain_hbm, gain_ref))
    rows, width = third_ref.shape
    slot = slot_col_ref[...]
    group = max(1, 2 * LANES // capacity)
    picked = jnp.zeros((rows, width), F32)
    for s in range(0, len(result_refs), group):
        results = jnp.concatenate([ref[...] for ref in result_refs[s : s + group]], axis=0)
        chosen = jnp.concatenate(
            [
                jnp.where(slot == iota(slot.shape, 1) + base, 1.0, 0.0).astype(BF)
                for base in range(s * capacity, (s + group) * capacity, LANES)
            ],
            axis=1,
        )
        picked = picked + dot(chosen, results)
    copies[0].wait()
    encoded = (third_ref[...].astype(F32) + layer_norm(picked, gain_ref[...])).astype(BF)
    turn = HALF * band_width
    out_ref[turn:, :] = encoded[: rows - turn, :]
    out_ref[:turn, :] = encoded[rows - turn :, :]


def call(kernel, outs, ins, places, scratch=(), limit=32, flops=0, size=None):
    spaces = {"s": pltpu.SMEM, "v": pltpu.VMEM, "h": pltpu.HBM, "a": pl.ANY}
    if size is None:
        size = sum(math.prod(a.shape) * a.dtype.itemsize for a in list(ins) + list(outs))
    results = pl.pallas_call(
        kernel,
        out_shape=outs,
        in_specs=[pl.BlockSpec(memory_space=spaces[p]) for p in places],
        out_specs=[pl.BlockSpec(memory_space=pltpu.VMEM)] * len(outs),
        scratch_shapes=list(scratch),
        compiler_params=pltpu.CompilerParams(vmem_limit_bytes=limit << 20),
        cost_estimate=pl.CostEstimate(flops=flops, bytes_accessed=size, transcendentals=0),
    )(*ins)
    return list(results)


def shape_of(*dims, dtype=BF):
    return jax.ShapeDtypeStruct(dims, dtype)


def swap(block, axis, bits):
    return lax.ppermute(block, axis, [(i, i ^ bits) for i in range(lax.axis_size(axis))])


def local(
    features,
    routes,
    qkv_regular,
    proj_regular,
    table_regular,
    gain_regular,
    mlp_up,
    mlp_down,
    gain_mlp,
    qkv_shifted,
    proj_shifted,
    table_shifted,
    gain_shifted,
    expert_in,
    expert_out,
    gain_expert,
):
    crop_count, height, band_width, width = features.shape
    rows = height * band_width
    band_count = lax.axis_size("band")
    band_index = lax.axis_index("band")
    experts = lax.axis_size("expert")
    capacity = 2 * rows // experts
    hidden = mlp_up.shape[1]
    strip = WIN * band_width
    tiles = width // LANES
    wide = LANES // (width // HEADS) * strip
    wide_halo = LANES // (width // HEADS) * 2 * WIN * HALF
    sent = height * HALF

    in_next = swap(expert_in[0], "band", 1)
    out_next = swap(expert_out[0], "band", 2)

    info = jnp.stack([band_index == 0, band_index == band_count - 1]).astype(I32)
    turn = HALF * band_width
    route_row = jnp.roll(routes.reshape(1, rows), -turn, axis=1) ^ lax.axis_index("expert")

    second, to_left, to_right = call(
        functools.partial(front_kernel, band_width),
        [shape_of(rows, width), shape_of(sent, width), shape_of(sent, width)],
        [
            table_regular.T,
            features.reshape(rows, width),
            qkv_regular,
            proj_regular,
            gain_regular.reshape(1, width),
            mlp_up,
            mlp_down,
            gain_mlp.reshape(1, width),
        ],
        "hhhhhhhh",
        [
            pltpu.VMEM((rows, width), BF),
            pltpu.VMEM((width, 3 * width), BF),
            pltpu.VMEM((width, width), BF),
            pltpu.VMEM((1, width), F32),
            pltpu.VMEM((width, hidden), BF),
            pltpu.VMEM((hidden, width), BF),
            pltpu.VMEM((1, width), F32),
            pltpu.VMEM(table_regular.shape[::-1], F32),
            pltpu.SemaphoreType.DMA((8,)),
            pltpu.VMEM((HEADS, 2 * LANES), F32),
            pltpu.VMEM((rows, 3 * width), BF),
            pltpu.VMEM((tiles, strip, wide), F32),
            pltpu.VMEM((rows, width), BF),
            pltpu.VMEM((rows, hidden), BF),
            pltpu.VMEM((rows, width), BF),
        ],
        limit=60,
        flops=2 * rows * width * (4 * width + 2 * hidden),
    )
    ring = range(band_count)
    from_right = lax.ppermute(to_left, "band", [(i, (i - 1) % band_count) for i in ring])
    from_left = lax.ppermute(to_right, "band", [(i, (i + 1) % band_count) for i in ring])
    qkv, bias, bias_halo, slot_row, wqkv, in_own, out_own = call(
        functools.partial(middle_kernel, band_width, experts, capacity),
        [
            shape_of(rows, 3 * width),
            shape_of(tiles, strip, wide, dtype=F32),
            shape_of(tiles, strip, wide_halo, dtype=F32),
            shape_of(8, rows, dtype=I32),
            shape_of(width, 3 * width),
            shape_of(2, *expert_in.shape[1:]),
            shape_of(2, *expert_out.shape[1:]),
        ],
        [
            info,
            second,
            route_row,
            table_shifted.T,
            qkv_shifted,
            expert_in[0],
            in_next,
            expert_out[0],
            out_next,
        ],
        "savhhhaha",
        [
            pltpu.VMEM(table_shifted.shape[::-1], F32),
            pltpu.VMEM((rows, width), BF),
            pltpu.SemaphoreType.DMA((7,)),
            pltpu.VMEM((HEADS, 2 * LANES), F32),
        ],
        flops=2 * rows * width * 3 * width,
    )
    from_left, from_right, in_own, out_own = lax.optimization_barrier(
        (from_left, from_right, in_own, out_own)
    )
    in_far = swap(in_own, "band", 2)
    out_far = swap(out_own, "band", 1)
    third, *outgoing = call(
        functools.partial(shifted_kernel, band_width, capacity),
        [shape_of(rows, width)] + [shape_of(capacity, width)] * experts,
        [
            info,
            qkv,
            second,
            from_left,
            from_right,
            wqkv,
            bias,
            bias_halo,
            slot_row,
            proj_shifted,
            gain_shifted.reshape(1, width),
        ],
        "svvvvvvvvhh",
        [
            pltpu.VMEM((2 * sent, 2 * width), BF),
            pltpu.VMEM((rows, width), BF),
            pltpu.VMEM((width, width), BF),
            pltpu.VMEM((1, width), F32),
            pltpu.SemaphoreType.DMA((2,)),
        ],
        flops=2 * rows * width * 4 * width,
    )
    weights = [in_own, in_far, out_own, out_far]

    def send(blocks, first):
        return [swap(block, "expert", first + k) for k, block in enumerate(blocks)]

    def compute(blocks):
        return call(
            functools.partial(expert_kernel, len(blocks)),
            [shape_of(capacity, width)] * len(blocks),
            blocks + weights,
            "v" * (len(blocks) + 4),
            flops=4 * len(blocks) * capacity * width * hidden,
        )

    far, most = experts // 2, 3 * experts // 4
    third_part = send(outgoing[far:most], far)
    slot_row, *third_part = lax.optimization_barrier(
        (slot_row, *third_part, *outgoing[most:])
    )
    slot_col = call(column_kernel, [shape_of(rows, LANES, dtype=I32)], [slot_row], "v")[0]
    fourth_part = send(third_part[most - far :], most)
    third_part = compute(third_part[: most - far])
    *third_part, = lax.optimization_barrier((*third_part, *outgoing[:far]))
    near = third_part[most - far :]
    near = near[:1] + send(near[1:], 1)
    back_third = send(third_part[: most - far], far)
    back_fourth = send(compute(fourth_part), most)
    half = far // 2
    first_part, second_part = compute(near[:half]), compute(near[half:])
    returned = (
        first_part[:1]
        + send(first_part[1:], 1)
        + send(second_part, half)
        + back_third
        + back_fourth
    )
    encoded = call(
        functools.partial(final_kernel, band_width, capacity),
        [shape_of(rows, width)],
        [third, slot_col, gain_expert.reshape(1, width)] + returned,
        "vvh" + "v" * experts,
        [pltpu.VMEM((1, width), F32), pltpu.SemaphoreType.DMA((1,))],
        flops=2 * rows * width * 2 * rows,
    )[0]
    return encoded.reshape(crop_count, height, band_width, width)


def solution(mesh):
    return jax.shard_map(
        local,
        mesh=mesh,
        in_specs=(
            P("expert", None, "band", None),
            P("expert", "band", None, None, None),
        )
        + (P(),) * 11
        + (
            P("expert", None, "band"),
            P("expert", "band", None),
            P(),
        ),
        out_specs=P("expert", None, "band", None),
        check_vma=False,
    )
```

```python
import functools
import math

import jax
import jax.numpy as jnp
from jax import lax
from jax.experimental import pallas as pl
from jax.experimental.pallas import tpu as pltpu
from jax.sharding import PartitionSpec as P

HEADS = 16
WIN = 8
HALF = WIN // 2
SPAN = 2 * WIN - 1
LANES = 128
LOG2E = math.log2(math.e)
CLOSED = -1e30
MASKED = -100.0 * LOG2E
BF = jnp.bfloat16
F32 = jnp.float32
I32 = jnp.int32

NN = (((1,), (0,)), ((), ()))
NT = (((1,), (1,)), ((), ()))


def dot(a, b, dims=NN):
    return lax.dot_general(a, b, dims, preferred_element_type=F32)


def iota(shape, dim):
    return lax.broadcasted_iota(I32, shape, dim)


def gelu(x):
    return 0.5 * x * (1.0 + lax.erf(x * math.sqrt(0.5)))


def layer_norm(values, gain):
    centre = jnp.mean(values, axis=-1, keepdims=True)
    offsets = values - centre
    spread = jnp.mean(offsets * offsets, axis=-1, keepdims=True)
    return offsets * lax.rsqrt(spread + 1e-05) * gain


def pick(row, idx):
    low = jnp.broadcast_to(row[:, :LANES], idx.shape)
    high = jnp.broadcast_to(row[:, LANES:], idx.shape)
    from_low = jnp.take_along_axis(
        low, jnp.minimum(idx, LANES - 1), axis=1, mode="promise_in_bounds"
    )
    from_high = jnp.take_along_axis(
        high, jnp.maximum(idx - LANES, 0), axis=1, mode="promise_in_bounds"
    )
    return jnp.where(idx < LANES, from_low, from_high)


def head_rows(table_ref, tab_ref):
    tab_ref[:, : table_ref.shape[1]] = table_ref[...] * LOG2E


def offset_index(row_p, col_p, row_q, col_q):
    return (row_p - row_q + WIN - 1) * SPAN + (col_p - col_q + WIN - 1)


def own_bias(tab_ref, bias_ref, band_width, shift):
    strip = WIN * band_width
    p, q = iota((strip, strip), 0), iota((strip, strip), 1)
    row_p, col_p = lax.div(p, band_width), lax.rem(p, band_width) + shift
    row_q, col_q = lax.div(q, band_width), lax.rem(q, band_width) + shift
    idx = offset_index(row_p, lax.rem(col_p, WIN), row_q, lax.rem(col_q, WIN))
    same = lax.div(col_p, WIN) == lax.div(col_q, WIN)
    for h in range(HEADS):
        row = tab_ref[h : h + 1, :]
        tile, part = divmod(h, 4)
        bias_ref[tile, :, part * strip : (part + 1) * strip] = jnp.where(
            same, pick(row, idx), CLOSED
        )


def halo_places(band_width):
    strip, halo = WIN * band_width, 2 * WIN * HALF
    p, q = iota((strip, 2 * halo), 0), iota((strip, 2 * halo), 1)
    row_p, col_p = lax.div(p, band_width), lax.rem(p, band_width) + HALF
    key = lax.rem(q, halo)
    right = key >= WIN * HALF
    cell = lax.rem(key, WIN * HALF)
    row_q = lax.div(cell, HALF)
    col_q = lax.rem(cell, HALF) + jnp.where(right, band_width + HALF, 0)
    return row_p, col_p, row_q, col_q, right, q < halo


def halo_bias(tab_ref, bias_ref, band_width, at_first, at_last):
    row_p, col_p, row_q, col_q, right, front = halo_places(band_width)
    idx = offset_index(row_p, lax.rem(col_p, WIN), row_q, lax.rem(col_q, WIN))
    same = lax.div(col_p, WIN) == lax.div(col_q, WIN)
    edge = jnp.where(right, at_last, at_first) > 0
    wide = front.shape[1]
    for pair in range(HEADS // 2):
        h = 2 * pair
        value = jnp.where(
            front, pick(tab_ref[h : h + 1, :], idx), pick(tab_ref[h + 1 : h + 2, :], idx)
        )
        value = jnp.where(same, value + jnp.where(edge, MASKED, 0.0), CLOSED)
        tile, part = divmod(pair, 2)
        bias_ref[tile, :, part * wide : (part + 1) * wide] = value


def head_masks(parts):
    lane_head = lax.div(iota((1, LANES), 1), LANES // parts)
    return [jnp.where(lane_head == h, 1.0, 0.0).astype(BF) for h in range(parts)]


def sum_columns(keys, parts):
    shape = (parts * keys, LANES)
    return jnp.where(
        lax.div(iota(shape, 0), keys) == lax.div(iota(shape, 1), LANES // parts), 1.0, 0.0
    ).astype(BF)


def spread(tops):
    lane_head = lax.div(iota((tops[0].shape[0], LANES), 1), LANES // len(tops))
    spread_out = tops[-1]
    for h in range(len(tops) - 2, -1, -1):
        spread_out = jnp.where(lane_head == h, tops[h], spread_out)
    return spread_out


def by_head(block, masks):
    return jnp.concatenate([block * mask for mask in masks], axis=0)


def fetch(sems, *pairs):
    copies = [pltpu.make_async_copy(a, b, sems.at[i]) for i, (a, b) in enumerate(pairs)]
    for copy in copies:
        copy.start()
    return copies


def front_kernel(
    band_width,
    table_hbm,
    x_hbm,
    wqkv_hbm,
    wproj_hbm,
    gain_hbm,
    up_hbm,
    down_hbm,
    gain_mlp_hbm,
    out_ref,
    left_ref,
    right_ref,
    x_ref,
    wqkv_ref,
    wproj_ref,
    gain_ref,
    up_ref,
    down_ref,
    gain_mlp_ref,
    table_ref,
    sems,
    tab_ref,
    qkv,
    bias,
    heads,
    act,
    second,
):
    rows, width = x_ref.shape
    strip = WIN * band_width
    head_dim = width // HEADS
    parts = LANES // head_dim
    copies = fetch(
        sems,
        (table_hbm, table_ref),
        (x_hbm, x_ref),
        (wqkv_hbm, wqkv_ref),
    )
    copies[0].wait()
    head_rows(table_ref, tab_ref)
    own_bias(tab_ref, bias, band_width, 0)
    copies[1].wait()
    copies[2].wait()
    copies = fetch(
        sems.at[3:],
        (wproj_hbm, wproj_ref),
        (gain_hbm, gain_ref),
        (up_hbm, up_ref),
        (down_hbm, down_ref),
        (gain_mlp_hbm, gain_mlp_ref),
    )
    x = x_ref[...]
    for part in range(3):
        cols = slice(part * width, (part + 1) * width)
        product = dot(x, wqkv_ref[:, cols])
        if part == 0:
            product = product * (LOG2E * head_dim**-0.5)
        qkv[:, cols] = product.astype(BF)
    masks = head_masks(parts)
    ones = sum_columns(strip, parts)

    def tile_step(t, carry):
        lanes = pl.ds(pl.multiple_of(t * LANES, LANES), LANES)
        lanes_k = pl.ds(pl.multiple_of(width + t * LANES, LANES), LANES)
        lanes_v = pl.ds(pl.multiple_of(2 * width + t * LANES, LANES), LANES)
        bias_tile = bias.at[t]
        for g in range(rows // strip):
            tokens = slice(g * strip, (g + 1) * strip)
            keys = by_head(qkv[tokens, lanes_k], masks)
            scores = dot(qkv[tokens, lanes], keys, NT) + bias_tile[...]
            probs = []
            for h in range(parts):
                s = scores[:, h * strip : (h + 1) * strip]
                probs.append(jnp.exp2(s - jnp.max(s, axis=-1, keepdims=True)).astype(BF))
            values = jnp.concatenate([by_head(qkv[tokens, lanes_v], masks), ones], axis=1)
            both = dot(jnp.concatenate(probs, axis=1), values)
            heads[tokens, lanes] = (both[:, :LANES] / both[:, LANES:]).astype(BF)
        return carry

    lax.fori_loop(0, width // LANES, tile_step, 0, unroll=True)
    for copy in copies:
        copy.wait()
    projected = dot(heads[...], wproj_ref[...])
    first = (x_ref[...].astype(F32) + layer_norm(projected, gain_ref[...])).astype(BF)
    act[...] = gelu(dot(first, up_ref[...])).astype(BF)
    dense = layer_norm(dot(act[...], down_ref[...]), gain_mlp_ref[...])
    second[...] = (first.astype(F32) + dense).astype(BF)
    turn = HALF * band_width
    rolled = jnp.concatenate([second[turn:, :], second[:turn, :]], axis=0)
    out_ref[...] = rolled
    sent = left_ref.shape[0]
    r, t = iota((sent, rows), 0), iota((sent, rows), 1)
    place = lax.div(r, HALF) * band_width + lax.rem(r, HALF)
    left_ref[...] = dot(jnp.where(t == place, 1.0, 0.0).astype(BF), rolled).astype(BF)
    place = place + (band_width - HALF)
    right_ref[...] = dot(jnp.where(t == place, 1.0, 0.0).astype(BF), rolled).astype(BF)


def column_kernel(slot_row_ref, slot_col_ref):
    rows = slot_row_ref.shape[1]
    slot = slot_row_ref[...]
    digit = iota(slot.shape, 0)
    parts = jnp.where(
        digit == 0, lax.rem(slot, LANES), jnp.where(digit == 1, lax.div(slot, LANES), 0)
    )
    same = jnp.where(iota((rows, rows), 0) == iota((rows, rows), 1), 1.0, 0.0).astype(BF)
    turned = dot(same, parts.astype(F32).astype(BF), NT)
    column = turned[:, 0:1] + turned[:, 1:2] * LANES
    slot_col_ref[...] = jnp.broadcast_to(column, slot_col_ref.shape).astype(I32)


def stack_kernel(in_first, in_second, out_first, out_second, in_pair, out_pair, sems):
    places = (in_pair.at[0], in_pair.at[1], out_pair.at[0], out_pair.at[1])
    for copy in fetch(sems, *zip((in_first, in_second, out_first, out_second), places)):
        copy.wait()


def middle_kernel(
    band_width,
    experts,
    capacity,
    info_ref,
    x_any,
    routes_ref,
    table_hbm,
    wqkv_hbm,
    qkv_ref,
    sums_ref,
    weights_ref,
    tops_ref,
    bias_halo_ref,
    slot_row_ref,
    wqkv_ref,
    table_ref,
    x_ref,
    sems,
    tab_ref,
    bias_ref,
):
    rows, width = x_ref.shape
    head_dim = width // HEADS
    strip = WIN * band_width
    parts = LANES // head_dim
    copies = fetch(
        sems,
        (table_hbm, table_ref),
        (wqkv_hbm, wqkv_ref),
        (x_any, x_ref),
    )
    copies[0].wait()
    head_rows(table_ref, tab_ref)
    own_bias(tab_ref, bias_ref, band_width, HALF)
    halo_bias(tab_ref, bias_halo_ref, band_width, info_ref[0], info_ref[1])
    routes = routes_ref[...]
    named = jnp.where(iota((experts, rows), 0) == routes, 1.0, 0.0)
    a, b = iota((rows, rows), 0), iota((rows, rows), 1)
    upto = jnp.where(a <= b, 1.0, 0.0).astype(BF)
    count = dot(named.astype(BF), upto)
    base = iota((experts, rows), 0).astype(F32) * capacity - 1.0
    slot = jnp.sum(named * (count + base), axis=0, keepdims=True)
    slot_row_ref[...] = jnp.broadcast_to(slot, slot_row_ref.shape).astype(I32)
    copies[1].wait()
    copies[2].wait()
    x = x_ref[...]
    for part in range(3):
        cols = slice(part * width, (part + 1) * width)
        product = dot(x, wqkv_ref[:, cols])
        if part == 0:
            product = product * (LOG2E * head_dim**-0.5)
        qkv_ref[:, cols] = product.astype(BF)
    masks = head_masks(parts)
    ones = sum_columns(strip, parts)
    p, q = iota((strip, strip), 0), iota((strip, strip), 1)
    turned = HALF * band_width
    apart = jnp.where((p < turned) != (q < turned), MASKED, 0.0)
    groups = rows // strip
    for t in range(width // LANES):
        lanes, lanes_k, lanes_v = (
            slice(part * width + t * LANES, part * width + (t + 1) * LANES) for part in range(3)
        )
        for g in range(groups):
            tokens = slice(g * strip, (g + 1) * strip)
            keys = by_head(qkv_ref[tokens, lanes_k], masks)
            scores = dot(qkv_ref[tokens, lanes], keys, NT) + bias_ref[t]
            probs, tops = [], []
            for h in range(parts):
                s = scores[:, h * strip : (h + 1) * strip]
                if g == groups - 1:
                    s = s + apart
                tops.append(jnp.max(s, axis=-1, keepdims=True))
                probs.append(jnp.exp2(s - tops[h]).astype(BF))
            values = jnp.concatenate([by_head(qkv_ref[tokens, lanes_v], masks), ones], axis=1)
            both = dot(jnp.concatenate(probs, axis=1), values)
            sums_ref[tokens, lanes] = both[:, :LANES]
            weights_ref[tokens, lanes] = both[:, LANES:]
            tops_ref[tokens, lanes] = spread(tops)


def shifted_kernel(
    band_width,
    capacity,
    info_ref,
    qkv_ref,
    x_ref,
    from_left_ref,
    from_right_ref,
    wqkv_ref,
    sums_ref,
    weights_ref,
    tops_ref,
    bias_halo_ref,
    slot_row_ref,
    wproj_hbm,
    gain_hbm,
    *rest,
):
    third_ref, *out_refs, halo_kv, heads, wproj_ref, gain_ref, sems = rest
    copies = fetch(sems, (wproj_hbm, wproj_ref), (gain_hbm, gain_ref))
    rows, width = x_ref.shape
    strip = WIN * band_width
    side = WIN * HALF
    halo = 2 * side
    groups = rows // strip
    head_dim = width // HEADS
    parts = LANES // head_dim
    arrived = jnp.concatenate(
        [
            ref[g * side : (g + 1) * side, :]
            for g in range(groups)
            for ref in (from_left_ref, from_right_ref)
        ],
        axis=0,
    )
    halo_kv[...] = dot(arrived, wqkv_ref[:, width:]).astype(BF)
    masks = head_masks(parts)
    ones = sum_columns(halo, parts)
    row_p, _, row_q, _, right, front = halo_places(band_width)
    edge = jnp.where(right, info_ref[1], info_ref[0]) > 0
    crossed = (row_p < HALF) != (row_q < HALF)
    apart_halo = jnp.where(jnp.logical_and(crossed, jnp.logical_not(edge)), MASKED, 0.0)
    wide = 2 * halo
    for t in range(width // LANES):
        lanes, lanes_k = (
            slice(part * width + t * LANES, part * width + (t + 1) * LANES) for part in range(2)
        )
        for g in range(groups):
            tokens = slice(g * strip, (g + 1) * strip)
            outside = slice(g * halo, (g + 1) * halo)
            keys = by_head(halo_kv[outside, lanes], masks)
            scores = dot(qkv_ref[tokens, lanes], keys, NT) + bias_halo_ref[t]
            probs, tops = [], []
            for pair in range(parts // 2):
                s = scores[:, pair * wide : (pair + 1) * wide]
                if g == groups - 1:
                    s = s + apart_halo
                first = jnp.max(jnp.where(front, s, CLOSED), axis=-1, keepdims=True)
                second = jnp.max(jnp.where(front, CLOSED, s), axis=-1, keepdims=True)
                tops += [first, second]
                probs.append(jnp.exp2(s - jnp.where(front, first, second)).astype(BF))
            values = jnp.concatenate([by_head(halo_kv[outside, lanes_k], masks), ones], axis=1)
            both = dot(jnp.concatenate(probs, axis=1), values)
            own_top, halo_top = tops_ref[tokens, lanes], spread(tops)
            top = jnp.maximum(own_top, halo_top)
            own, other = jnp.exp2(own_top - top), jnp.exp2(halo_top - top)
            total = sums_ref[tokens, lanes] * own + both[:, :LANES] * other
            weight = weights_ref[tokens, lanes] * own + both[:, LANES:] * other
            heads[tokens, lanes] = (total / weight).astype(BF)
    for copy in copies:
        copy.wait()
    projected = dot(heads[...], wproj_ref[...])
    third = (x_ref[...].astype(F32) + layer_norm(projected, gain_ref[...])).astype(BF)
    third_ref[...] = third
    slot = slot_row_ref[0:1, :]
    group = max(1, 2 * LANES // capacity)
    for s in range(0, len(out_refs), group):
        places = iota((group * capacity, rows), 0) + s * capacity
        sent = dot(jnp.where(places == slot, 1.0, 0.0).astype(BF), third).astype(BF)
        for k in range(group):
            out_refs[s + k][...] = sent[k * capacity : (k + 1) * capacity, :]


def expert_kernel(amount, *refs):
    x_refs, (in_own, in_far, out_own, out_far), out_refs = (
        refs[:amount],
        refs[amount : amount + 4],
        refs[amount + 4 :],
    )
    in_refs = (in_own.at[0], in_own.at[1], in_far.at[0], in_far.at[1])
    out_w_refs = (out_own.at[0], out_far.at[0], out_own.at[1], out_far.at[1])
    x = jnp.concatenate([ref[...] for ref in x_refs], axis=0)
    total = jnp.zeros(x.shape, F32)
    for w_in, w_out in zip(in_refs, out_w_refs):
        total = total + dot(gelu(dot(x, w_in[...])).astype(BF), w_out[...])
    each = x_refs[0].shape[0]
    for k, ref in enumerate(out_refs):
        ref[...] = total[k * each : (k + 1) * each, :].astype(BF)


def final_kernel(band_width, capacity, third_ref, slot_col_ref, gain_hbm, *rest):
    *result_refs, out_ref, gain_ref, sems = rest
    copies = fetch(sems, (gain_hbm, gain_ref))
    rows, width = third_ref.shape
    slot = slot_col_ref[...]
    group = max(1, 2 * LANES // capacity)
    picked = jnp.zeros((rows, width), F32)
    for s in range(0, len(result_refs), group):
        results = jnp.concatenate([ref[...] for ref in result_refs[s : s + group]], axis=0)
        chosen = jnp.concatenate(
            [
                jnp.where(slot == iota(slot.shape, 1) + base, 1.0, 0.0).astype(BF)
                for base in range(s * capacity, (s + group) * capacity, LANES)
            ],
            axis=1,
        )
        picked = picked + dot(chosen, results)
    copies[0].wait()
    encoded = (third_ref[...].astype(F32) + layer_norm(picked, gain_ref[...])).astype(BF)
    turn = HALF * band_width
    out_ref[turn:, :] = encoded[: rows - turn, :]
    out_ref[:turn, :] = encoded[rows - turn :, :]


def call(kernel, outs, ins, places, scratch=(), limit=32, flops=0, size=None):
    spaces = {"s": pltpu.SMEM, "v": pltpu.VMEM, "h": pltpu.HBM, "a": pl.ANY}
    if size is None:
        size = sum(math.prod(a.shape) * a.dtype.itemsize for a in list(ins) + list(outs))
    results = pl.pallas_call(
        kernel,
        out_shape=outs,
        in_specs=[pl.BlockSpec(memory_space=spaces[p]) for p in places],
        out_specs=[pl.BlockSpec(memory_space=pltpu.VMEM)] * len(outs),
        scratch_shapes=list(scratch),
        compiler_params=pltpu.CompilerParams(vmem_limit_bytes=int(limit * 2**20)),
        cost_estimate=pl.CostEstimate(flops=flops, bytes_accessed=size, transcendentals=0),
    )(*ins)
    return list(results)


def shape_of(*dims, dtype=BF):
    return jax.ShapeDtypeStruct(dims, dtype)


def swap(block, axis, bits):
    return lax.ppermute(block, axis, [(i, i ^ bits) for i in range(lax.axis_size(axis))])


def local(
    features,
    routes,
    qkv_regular,
    proj_regular,
    table_regular,
    gain_regular,
    mlp_up,
    mlp_down,
    gain_mlp,
    qkv_shifted,
    proj_shifted,
    table_shifted,
    gain_shifted,
    expert_in,
    expert_out,
    gain_expert,
):
    crop_count, height, band_width, width = features.shape
    rows = height * band_width
    band_count = lax.axis_size("band")
    band_index = lax.axis_index("band")
    experts = lax.axis_size("expert")
    capacity = 2 * rows // experts
    hidden = mlp_up.shape[1]
    strip = WIN * band_width
    tiles = width // LANES
    wide = LANES // (width // HEADS) * strip
    wide_halo = LANES // (width // HEADS) * 2 * WIN * HALF
    sent = height * HALF

    in_next = swap(expert_in[0], "band", 1)
    out_next = swap(expert_out[0], "band", 2)

    info = jnp.stack([band_index == 0, band_index == band_count - 1]).astype(I32)
    turn = HALF * band_width
    route_row = jnp.roll(routes.reshape(1, rows), -turn, axis=1) ^ lax.axis_index("expert")

    second, to_left, to_right = call(
        functools.partial(front_kernel, band_width),
        [shape_of(rows, width), shape_of(sent, width), shape_of(sent, width)],
        [
            table_regular.T,
            features.reshape(rows, width),
            qkv_regular,
            proj_regular,
            gain_regular.reshape(1, width),
            mlp_up,
            mlp_down,
            gain_mlp.reshape(1, width),
        ],
        "hhhhhhhh",
        [
            pltpu.VMEM((rows, width), BF),
            pltpu.VMEM((width, 3 * width), BF),
            pltpu.VMEM((width, width), BF),
            pltpu.VMEM((1, width), F32),
            pltpu.VMEM((width, hidden), BF),
            pltpu.VMEM((hidden, width), BF),
            pltpu.VMEM((1, width), F32),
            pltpu.VMEM(table_regular.shape[::-1], F32),
            pltpu.SemaphoreType.DMA((8,)),
            pltpu.VMEM((HEADS, 2 * LANES), F32),
            pltpu.VMEM((rows, 3 * width), BF),
            pltpu.VMEM((tiles, strip, wide), F32),
            pltpu.VMEM((rows, width), BF),
            pltpu.VMEM((rows, hidden), BF),
            pltpu.VMEM((rows, width), BF),
        ],
        limit=60,
        flops=2 * rows * width * (4 * width + 2 * hidden),
    )
    ring = range(band_count)
    from_right = lax.ppermute(to_left, "band", [(i, (i - 1) % band_count) for i in ring])
    from_left = lax.ppermute(to_right, "band", [(i, (i + 1) % band_count) for i in ring])
    qkv, *own_heads, bias_halo, slot_row, wqkv = call(
        functools.partial(middle_kernel, band_width, experts, capacity),
        [
            shape_of(rows, 3 * width),
            shape_of(rows, width, dtype=F32),
            shape_of(rows, width, dtype=F32),
            shape_of(rows, width, dtype=F32),
            shape_of(tiles, strip, wide_halo, dtype=F32),
            shape_of(8, rows, dtype=I32),
            shape_of(width, 3 * width),
        ],
        [
            info,
            second,
            route_row,
            table_shifted.T,
            qkv_shifted,
        ],
        "savhh",
        [
            pltpu.VMEM(table_shifted.shape[::-1], F32),
            pltpu.VMEM((rows, width), BF),
            pltpu.SemaphoreType.DMA((3,)),
            pltpu.VMEM((HEADS, 2 * LANES), F32),
            pltpu.VMEM((tiles, strip, wide), F32),
        ],
        limit=46.5,
        flops=2 * rows * width * 3 * width,
    )
    from_left, from_right, bias_halo, in_next, out_next = lax.optimization_barrier(
        (from_left, from_right, bias_halo, in_next, out_next)
    )
    in_own, out_own = call(
        stack_kernel,
        [shape_of(2, *expert_in.shape[1:]), shape_of(2, *expert_out.shape[1:])],
        [expert_in[0], in_next, expert_out[0], out_next],
        "vvvv",
        [pltpu.SemaphoreType.DMA((4,))],
        limit=8,
    )
    in_far = swap(in_own, "band", 2)
    out_far = swap(out_own, "band", 1)
    third, *outgoing = call(
        functools.partial(shifted_kernel, band_width, capacity),
        [shape_of(rows, width)] + [shape_of(capacity, width)] * experts,
        [
            info,
            qkv,
            second,
            from_left,
            from_right,
            wqkv,
            *own_heads,
            bias_halo,
            slot_row,
            proj_shifted,
            gain_shifted.reshape(1, width),
        ],
        "svvvvvvvvvvhh",
        [
            pltpu.VMEM((2 * sent, 2 * width), BF),
            pltpu.VMEM((rows, width), BF),
            pltpu.VMEM((width, width), BF),
            pltpu.VMEM((1, width), F32),
            pltpu.SemaphoreType.DMA((2,)),
        ],
        flops=2 * rows * width * 4 * width,
    )
    weights = [in_own, in_far, out_own, out_far]

    def send(blocks, first):
        return [swap(block, "expert", first + k) for k, block in enumerate(blocks)]

    def compute(blocks):
        return call(
            functools.partial(expert_kernel, len(blocks)),
            [shape_of(capacity, width)] * len(blocks),
            blocks + weights,
            "v" * (len(blocks) + 4),
            flops=4 * len(blocks) * capacity * width * hidden,
        )

    far, most = experts // 2, 3 * experts // 4
    third_part = send(outgoing[far:most], far)
    slot_row, *third_part = lax.optimization_barrier(
        (slot_row, *third_part, *outgoing[most:])
    )
    slot_col = call(column_kernel, [shape_of(rows, LANES, dtype=I32)], [slot_row], "v")[0]
    fourth_part = send(third_part[most - far :], most)
    third_part = compute(third_part[: most - far])
    *third_part, = lax.optimization_barrier((*third_part, *outgoing[:far]))
    near = third_part[most - far :]
    near = near[:1] + send(near[1:], 1)
    back_third = send(third_part[: most - far], far)
    back_fourth = send(compute(fourth_part), most)
    half = far // 2
    first_part, second_part = compute(near[:half]), compute(near[half:])
    returned = (
        first_part[:1]
        + send(first_part[1:], 1)
        + send(second_part, half)
        + back_third
        + back_fourth
    )
    encoded = call(
        functools.partial(final_kernel, band_width, capacity),
        [shape_of(rows, width)],
        [third, slot_col, gain_expert.reshape(1, width)] + returned,
        "vvh" + "v" * experts,
        [pltpu.VMEM((1, width), F32), pltpu.SemaphoreType.DMA((1,))],
        flops=2 * rows * width * 2 * rows,
    )[0]
    return encoded.reshape(crop_count, height, band_width, width)


def solution(mesh):
    return jax.shard_map(
        local,
        mesh=mesh,
        in_specs=(
            P("expert", None, "band", None),
            P("expert", "band", None, None, None),
        )
        + (P(),) * 11
        + (
            P("expert", None, "band"),
            P("expert", "band", None),
            P(),
        ),
        out_specs=P("expert", None, "band", None),
        check_vma=False,
    )
```

```python
import functools
import math

import jax
import jax.numpy as jnp
from jax import lax
from jax.experimental import pallas as pl
from jax.experimental.pallas import tpu as pltpu
from jax.sharding import PartitionSpec as P

HEADS = 16
WIN = 8
HALF = WIN // 2
SPAN = 2 * WIN - 1
LANES = 128
LOG2E = math.log2(math.e)
CLOSED = -1e30
MASKED = -100.0 * LOG2E
BF = jnp.bfloat16
F32 = jnp.float32
I32 = jnp.int32

NN = (((1,), (0,)), ((), ()))
NT = (((1,), (1,)), ((), ()))


def dot(a, b, dims=NN):
    return lax.dot_general(a, b, dims, preferred_element_type=F32)


def iota(shape, dim):
    return lax.broadcasted_iota(I32, shape, dim)


def gelu(x):
    return 0.5 * x * (1.0 + lax.erf(x * math.sqrt(0.5)))


def layer_norm(values, gain):
    centre = jnp.mean(values, axis=-1, keepdims=True)
    offsets = values - centre
    spread = jnp.mean(offsets * offsets, axis=-1, keepdims=True)
    return offsets * lax.rsqrt(spread + 1e-05) * gain


def pick(row, idx):
    low = jnp.broadcast_to(row[:, :LANES], idx.shape)
    high = jnp.broadcast_to(row[:, LANES:], idx.shape)
    from_low = jnp.take_along_axis(
        low, jnp.minimum(idx, LANES - 1), axis=1, mode="promise_in_bounds"
    )
    from_high = jnp.take_along_axis(
        high, jnp.maximum(idx - LANES, 0), axis=1, mode="promise_in_bounds"
    )
    return jnp.where(idx < LANES, from_low, from_high)


def head_rows(table_ref, tab_ref):
    tab_ref[:, : table_ref.shape[1]] = table_ref[...] * LOG2E


def offset_index(row_p, col_p, row_q, col_q):
    return (row_p - row_q + WIN - 1) * SPAN + (col_p - col_q + WIN - 1)


def own_bias(tab_ref, bias_ref, band_width, shift):
    strip = WIN * band_width
    p, q = iota((strip, strip), 0), iota((strip, strip), 1)
    row_p, col_p = lax.div(p, band_width), lax.rem(p, band_width) + shift
    row_q, col_q = lax.div(q, band_width), lax.rem(q, band_width) + shift
    idx = offset_index(row_p, lax.rem(col_p, WIN), row_q, lax.rem(col_q, WIN))
    same = lax.div(col_p, WIN) == lax.div(col_q, WIN)
    for h in range(HEADS):
        row = tab_ref[h : h + 1, :]
        tile, part = divmod(h, 4)
        bias_ref[tile, :, part * strip : (part + 1) * strip] = jnp.where(
            same, pick(row, idx), CLOSED
        )


def halo_places(band_width):
    strip, halo = WIN * band_width, 2 * WIN * HALF
    p, q = iota((strip, 2 * halo), 0), iota((strip, 2 * halo), 1)
    row_p, col_p = lax.div(p, band_width), lax.rem(p, band_width) + HALF
    key = lax.rem(q, halo)
    right = key >= WIN * HALF
    cell = lax.rem(key, WIN * HALF)
    row_q = lax.div(cell, HALF)
    col_q = lax.rem(cell, HALF) + jnp.where(right, band_width + HALF, 0)
    return row_p, col_p, row_q, col_q, right, q < halo


def halo_bias(tab_ref, bias_ref, band_width, at_first, at_last):
    row_p, col_p, row_q, col_q, right, front = halo_places(band_width)
    idx = offset_index(row_p, lax.rem(col_p, WIN), row_q, lax.rem(col_q, WIN))
    same = lax.div(col_p, WIN) == lax.div(col_q, WIN)
    edge = jnp.where(right, at_last, at_first) > 0
    wide = front.shape[1]
    for pair in range(HEADS // 2):
        h = 2 * pair
        value = jnp.where(
            front, pick(tab_ref[h : h + 1, :], idx), pick(tab_ref[h + 1 : h + 2, :], idx)
        )
        value = jnp.where(same, value + jnp.where(edge, MASKED, 0.0), CLOSED)
        tile, part = divmod(pair, 2)
        bias_ref[tile, :, part * wide : (part + 1) * wide] = value


def head_masks(parts):
    lane_head = lax.div(iota((1, LANES), 1), LANES // parts)
    return [jnp.where(lane_head == h, 1.0, 0.0).astype(BF) for h in range(parts)]


def sum_columns(keys, parts):
    shape = (parts * keys, LANES)
    return jnp.where(
        lax.div(iota(shape, 0), keys) == lax.div(iota(shape, 1), LANES // parts), 1.0, 0.0
    ).astype(BF)


def spread(tops):
    lane_head = lax.div(iota((tops[0].shape[0], LANES), 1), LANES // len(tops))
    spread_out = tops[-1]
    for h in range(len(tops) - 2, -1, -1):
        spread_out = jnp.where(lane_head == h, tops[h], spread_out)
    return spread_out


def by_head(block, masks):
    return jnp.concatenate([block * mask for mask in masks], axis=0)


def fetch(sems, *pairs):
    copies = [pltpu.make_async_copy(a, b, sems.at[i]) for i, (a, b) in enumerate(pairs)]
    for copy in copies:
        copy.start()
    return copies


def front_kernel(
    band_width,
    table_hbm,
    x_hbm,
    wqkv_hbm,
    wproj_hbm,
    gain_hbm,
    up_hbm,
    down_hbm,
    gain_mlp_hbm,
    out_ref,
    left_ref,
    right_ref,
    x_ref,
    wqkv_ref,
    wproj_ref,
    gain_ref,
    up_ref,
    down_ref,
    gain_mlp_ref,
    table_ref,
    sems,
    tab_ref,
    qkv,
    bias,
    heads,
    act,
    second,
):
    rows, width = x_ref.shape
    strip = WIN * band_width
    head_dim = width // HEADS
    parts = LANES // head_dim
    copies = fetch(
        sems,
        (table_hbm, table_ref),
        (x_hbm, x_ref),
        (wqkv_hbm, wqkv_ref),
    )
    copies[0].wait()
    head_rows(table_ref, tab_ref)
    own_bias(tab_ref, bias, band_width, 0)
    copies[1].wait()
    copies[2].wait()
    copies = fetch(
        sems.at[3:],
        (wproj_hbm, wproj_ref),
        (gain_hbm, gain_ref),
        (up_hbm, up_ref),
        (down_hbm, down_ref),
        (gain_mlp_hbm, gain_mlp_ref),
    )
    x = x_ref[...]
    for part in range(3):
        cols = slice(part * width, (part + 1) * width)
        product = dot(x, wqkv_ref[:, cols])
        if part == 0:
            product = product * (LOG2E * head_dim**-0.5)
        qkv[:, cols] = product.astype(BF)
    masks = head_masks(parts)
    ones = sum_columns(strip, parts)

    def tile_step(t, carry):
        lanes = pl.ds(pl.multiple_of(t * LANES, LANES), LANES)
        lanes_k = pl.ds(pl.multiple_of(width + t * LANES, LANES), LANES)
        lanes_v = pl.ds(pl.multiple_of(2 * width + t * LANES, LANES), LANES)
        bias_tile = bias.at[t]
        for g in range(rows // strip):
            tokens = slice(g * strip, (g + 1) * strip)
            keys = by_head(qkv[tokens, lanes_k], masks)
            scores = dot(qkv[tokens, lanes], keys, NT) + bias_tile[...]
            probs = []
            for h in range(parts):
                s = scores[:, h * strip : (h + 1) * strip]
                probs.append(jnp.exp2(s - jnp.max(s, axis=-1, keepdims=True)).astype(BF))
            values = jnp.concatenate([by_head(qkv[tokens, lanes_v], masks), ones], axis=1)
            both = dot(jnp.concatenate(probs, axis=1), values)
            heads[tokens, lanes] = (both[:, :LANES] / both[:, LANES:]).astype(BF)
        return carry

    lax.fori_loop(0, width // LANES, tile_step, 0, unroll=True)
    for copy in copies:
        copy.wait()
    projected = dot(heads[...], wproj_ref[...])
    first = (x_ref[...].astype(F32) + layer_norm(projected, gain_ref[...])).astype(BF)
    act[...] = gelu(dot(first, up_ref[...])).astype(BF)
    dense = layer_norm(dot(act[...], down_ref[...]), gain_mlp_ref[...])
    second[...] = (first.astype(F32) + dense).astype(BF)
    turn = HALF * band_width
    rolled = jnp.concatenate([second[turn:, :], second[:turn, :]], axis=0)
    out_ref[...] = rolled
    sent = left_ref.shape[0]
    r, t = iota((sent, rows), 0), iota((sent, rows), 1)
    place = lax.div(r, HALF) * band_width + lax.rem(r, HALF)
    left_ref[...] = dot(jnp.where(t == place, 1.0, 0.0).astype(BF), rolled).astype(BF)
    place = place + (band_width - HALF)
    right_ref[...] = dot(jnp.where(t == place, 1.0, 0.0).astype(BF), rolled).astype(BF)


def column_kernel(slot_row_ref, slot_col_ref):
    rows = slot_row_ref.shape[1]
    slot = slot_row_ref[...]
    digit = iota(slot.shape, 0)
    parts = jnp.where(
        digit == 0, lax.rem(slot, LANES), jnp.where(digit == 1, lax.div(slot, LANES), 0)
    )
    same = jnp.where(iota((rows, rows), 0) == iota((rows, rows), 1), 1.0, 0.0).astype(BF)
    turned = dot(same, parts.astype(F32).astype(BF), NT)
    column = turned[:, 0:1] + turned[:, 1:2] * LANES
    slot_col_ref[...] = jnp.broadcast_to(column, slot_col_ref.shape).astype(I32)


def stack_kernel(in_first, in_second, out_first, out_second, in_pair, out_pair, sems):
    places = (in_pair.at[0], in_pair.at[1], out_pair.at[0], out_pair.at[1])
    for copy in fetch(sems, *zip((in_first, in_second, out_first, out_second), places)):
        copy.wait()


def middle_kernel(
    band_width,
    experts,
    capacity,
    info_ref,
    x_any,
    routes_ref,
    table_hbm,
    wqkv_hbm,
    qkv_ref,
    sums_ref,
    weights_ref,
    tops_ref,
    bias_halo_ref,
    slot_row_ref,
    wqkv_ref,
    table_ref,
    x_ref,
    sems,
    tab_ref,
    bias_ref,
):
    rows, width = x_ref.shape
    head_dim = width // HEADS
    strip = WIN * band_width
    parts = LANES // head_dim
    copies = fetch(
        sems,
        (table_hbm, table_ref),
        (wqkv_hbm, wqkv_ref),
        (x_any, x_ref),
    )
    copies[0].wait()
    head_rows(table_ref, tab_ref)
    own_bias(tab_ref, bias_ref, band_width, HALF)
    halo_bias(tab_ref, bias_halo_ref, band_width, info_ref[0], info_ref[1])
    routes = routes_ref[...]
    named = jnp.where(iota((experts, rows), 0) == routes, 1.0, 0.0)
    a, b = iota((rows, rows), 0), iota((rows, rows), 1)
    upto = jnp.where(a <= b, 1.0, 0.0).astype(BF)
    count = dot(named.astype(BF), upto)
    base = iota((experts, rows), 0).astype(F32) * capacity - 1.0
    slot = jnp.sum(named * (count + base), axis=0, keepdims=True)
    slot_row_ref[...] = jnp.broadcast_to(slot, slot_row_ref.shape).astype(I32)
    copies[1].wait()
    copies[2].wait()
    x = x_ref[...]
    for part in range(3):
        cols = slice(part * width, (part + 1) * width)
        product = dot(x, wqkv_ref[:, cols])
        if part == 0:
            product = product * (LOG2E * head_dim**-0.5)
        qkv_ref[:, cols] = product.astype(BF)
    masks = head_masks(parts)
    ones = sum_columns(strip, parts)
    p, q = iota((strip, strip), 0), iota((strip, strip), 1)
    turned = HALF * band_width
    apart = jnp.where((p < turned) != (q < turned), MASKED, 0.0)
    groups = rows // strip
    for t in range(width // LANES):
        lanes, lanes_k, lanes_v = (
            slice(part * width + t * LANES, part * width + (t + 1) * LANES) for part in range(3)
        )
        for g in range(groups):
            tokens = slice(g * strip, (g + 1) * strip)
            keys = by_head(qkv_ref[tokens, lanes_k], masks)
            scores = dot(qkv_ref[tokens, lanes], keys, NT) + bias_ref[t]
            probs, tops = [], []
            for h in range(parts):
                s = scores[:, h * strip : (h + 1) * strip]
                if g == groups - 1:
                    s = s + apart
                tops.append(jnp.max(s, axis=-1, keepdims=True))
                probs.append(jnp.exp2(s - tops[h]).astype(BF))
            values = jnp.concatenate([by_head(qkv_ref[tokens, lanes_v], masks), ones], axis=1)
            both = dot(jnp.concatenate(probs, axis=1), values)
            sums_ref[tokens, lanes] = both[:, :LANES]
            weights_ref[tokens, lanes] = both[:, LANES:]
            tops_ref[tokens, lanes] = spread(tops)


def shifted_kernel(
    band_width,
    capacity,
    info_ref,
    qkv_ref,
    x_any,
    from_left_ref,
    from_right_ref,
    wqkv_ref,
    sums_ref,
    weights_ref,
    tops_ref,
    bias_halo_ref,
    slot_row_ref,
    wproj_hbm,
    gain_hbm,
    *rest,
):
    third_ref, *out_refs, halo_kv, heads, wproj_ref, gain_ref, x_ref, sems = rest
    copies = fetch(sems, (wproj_hbm, wproj_ref), (gain_hbm, gain_ref), (x_any, x_ref))
    rows, width = x_ref.shape
    strip = WIN * band_width
    side = WIN * HALF
    halo = 2 * side
    groups = rows // strip
    head_dim = width // HEADS
    parts = LANES // head_dim
    arrived = jnp.concatenate(
        [
            ref[g * side : (g + 1) * side, :]
            for g in range(groups)
            for ref in (from_left_ref, from_right_ref)
        ],
        axis=0,
    )
    halo_kv[...] = dot(arrived, wqkv_ref[:, width:]).astype(BF)
    masks = head_masks(parts)
    ones = sum_columns(halo, parts)
    row_p, _, row_q, _, right, front = halo_places(band_width)
    edge = jnp.where(right, info_ref[1], info_ref[0]) > 0
    crossed = (row_p < HALF) != (row_q < HALF)
    apart_halo = jnp.where(jnp.logical_and(crossed, jnp.logical_not(edge)), MASKED, 0.0)
    wide = 2 * halo
    for t in range(width // LANES):
        lanes, lanes_k = (
            slice(part * width + t * LANES, part * width + (t + 1) * LANES) for part in range(2)
        )
        for g in range(groups):
            tokens = slice(g * strip, (g + 1) * strip)
            outside = slice(g * halo, (g + 1) * halo)
            keys = by_head(halo_kv[outside, lanes], masks)
            scores = dot(qkv_ref[tokens, lanes], keys, NT) + bias_halo_ref[t]
            probs, tops = [], []
            for pair in range(parts // 2):
                s = scores[:, pair * wide : (pair + 1) * wide]
                if g == groups - 1:
                    s = s + apart_halo
                first = jnp.max(jnp.where(front, s, CLOSED), axis=-1, keepdims=True)
                second = jnp.max(jnp.where(front, CLOSED, s), axis=-1, keepdims=True)
                tops += [first, second]
                probs.append(jnp.exp2(s - jnp.where(front, first, second)).astype(BF))
            values = jnp.concatenate([by_head(halo_kv[outside, lanes_k], masks), ones], axis=1)
            both = dot(jnp.concatenate(probs, axis=1), values)
            own_top, halo_top = tops_ref[tokens, lanes], spread(tops)
            top = jnp.maximum(own_top, halo_top)
            own, other = jnp.exp2(own_top - top), jnp.exp2(halo_top - top)
            total = sums_ref[tokens, lanes] * own + both[:, :LANES] * other
            weight = weights_ref[tokens, lanes] * own + both[:, LANES:] * other
            heads[tokens, lanes] = (total / weight).astype(BF)
    for copy in copies:
        copy.wait()
    projected = dot(heads[...], wproj_ref[...])
    third = (x_ref[...].astype(F32) + layer_norm(projected, gain_ref[...])).astype(BF)
    third_ref[...] = third
    slot = slot_row_ref[0:1, :]
    group = max(1, 2 * LANES // capacity)
    for s in range(0, len(out_refs), group):
        places = iota((group * capacity, rows), 0) + s * capacity
        sent = dot(jnp.where(places == slot, 1.0, 0.0).astype(BF), third).astype(BF)
        for k in range(group):
            out_refs[s + k][...] = sent[k * capacity : (k + 1) * capacity, :]


def expert_kernel(amount, *refs):
    x_refs, (in_own, in_far, out_own, out_far), out_refs = (
        refs[:amount],
        refs[amount : amount + 4],
        refs[amount + 4 :],
    )
    in_refs = (in_own.at[0], in_own.at[1], in_far.at[0], in_far.at[1])
    out_w_refs = (out_own.at[0], out_far.at[0], out_own.at[1], out_far.at[1])
    x = jnp.concatenate([ref[...] for ref in x_refs], axis=0)
    total = jnp.zeros(x.shape, F32)
    for w_in, w_out in zip(in_refs, out_w_refs):
        total = total + dot(gelu(dot(x, w_in[...])).astype(BF), w_out[...])
    each = x_refs[0].shape[0]
    for k, ref in enumerate(out_refs):
        ref[...] = total[k * each : (k + 1) * each, :].astype(BF)


def final_kernel(band_width, capacity, third_ref, slot_col_ref, gain_hbm, *rest):
    *result_refs, out_ref, gain_ref, sems = rest
    copies = fetch(sems, (gain_hbm, gain_ref))
    rows, width = third_ref.shape
    slot = slot_col_ref[...]
    group = max(1, 2 * LANES // capacity)
    picked = jnp.zeros((rows, width), F32)
    for s in range(0, len(result_refs), group):
        results = jnp.concatenate([ref[...] for ref in result_refs[s : s + group]], axis=0)
        chosen = jnp.concatenate(
            [
                jnp.where(slot == iota(slot.shape, 1) + base, 1.0, 0.0).astype(BF)
                for base in range(s * capacity, (s + group) * capacity, LANES)
            ],
            axis=1,
        )
        picked = picked + dot(chosen, results)
    copies[0].wait()
    encoded = (third_ref[...].astype(F32) + layer_norm(picked, gain_ref[...])).astype(BF)
    turn = HALF * band_width
    out_ref[turn:, :] = encoded[: rows - turn, :]
    out_ref[:turn, :] = encoded[rows - turn :, :]


def call(kernel, outs, ins, places, scratch=(), limit=32, flops=0, size=None):
    spaces = {"s": pltpu.SMEM, "v": pltpu.VMEM, "h": pltpu.HBM, "a": pl.ANY}
    if size is None:
        size = sum(math.prod(a.shape) * a.dtype.itemsize for a in list(ins) + list(outs))
    results = pl.pallas_call(
        kernel,
        out_shape=outs,
        in_specs=[pl.BlockSpec(memory_space=spaces[p]) for p in places],
        out_specs=[pl.BlockSpec(memory_space=pltpu.VMEM)] * len(outs),
        scratch_shapes=list(scratch),
        compiler_params=pltpu.CompilerParams(vmem_limit_bytes=int(limit * 2**20)),
        cost_estimate=pl.CostEstimate(flops=flops, bytes_accessed=size, transcendentals=0),
    )(*ins)
    return list(results)


def shape_of(*dims, dtype=BF):
    return jax.ShapeDtypeStruct(dims, dtype)


def swap(block, axis, bits):
    return lax.ppermute(block, axis, [(i, i ^ bits) for i in range(lax.axis_size(axis))])


def local(
    features,
    routes,
    qkv_regular,
    proj_regular,
    table_regular,
    gain_regular,
    mlp_up,
    mlp_down,
    gain_mlp,
    qkv_shifted,
    proj_shifted,
    table_shifted,
    gain_shifted,
    expert_in,
    expert_out,
    gain_expert,
):
    crop_count, height, band_width, width = features.shape
    rows = height * band_width
    band_count = lax.axis_size("band")
    band_index = lax.axis_index("band")
    experts = lax.axis_size("expert")
    capacity = 2 * rows // experts
    hidden = mlp_up.shape[1]
    strip = WIN * band_width
    tiles = width // LANES
    wide = LANES // (width // HEADS) * strip
    wide_halo = LANES // (width // HEADS) * 2 * WIN * HALF
    sent = height * HALF

    in_next = swap(expert_in[0], "band", 1)
    out_next = swap(expert_out[0], "band", 2)

    info = jnp.stack([band_index == 0, band_index == band_count - 1]).astype(I32)
    turn = HALF * band_width
    route_row = jnp.roll(routes.reshape(1, rows), -turn, axis=1) ^ lax.axis_index("expert")

    second, to_left, to_right = call(
        functools.partial(front_kernel, band_width),
        [shape_of(rows, width), shape_of(sent, width), shape_of(sent, width)],
        [
            table_regular.T,
            features.reshape(rows, width),
            qkv_regular,
            proj_regular,
            gain_regular.reshape(1, width),
            mlp_up,
            mlp_down,
            gain_mlp.reshape(1, width),
        ],
        "hhhhhhhh",
        [
            pltpu.VMEM((rows, width), BF),
            pltpu.VMEM((width, 3 * width), BF),
            pltpu.VMEM((width, width), BF),
            pltpu.VMEM((1, width), F32),
            pltpu.VMEM((width, hidden), BF),
            pltpu.VMEM((hidden, width), BF),
            pltpu.VMEM((1, width), F32),
            pltpu.VMEM(table_regular.shape[::-1], F32),
            pltpu.SemaphoreType.DMA((8,)),
            pltpu.VMEM((HEADS, 2 * LANES), F32),
            pltpu.VMEM((rows, 3 * width), BF),
            pltpu.VMEM((tiles, strip, wide), F32),
            pltpu.VMEM((rows, width), BF),
            pltpu.VMEM((rows, hidden), BF),
            pltpu.VMEM((rows, width), BF),
        ],
        limit=60,
        flops=2 * rows * width * (4 * width + 2 * hidden),
    )
    ring = range(band_count)
    from_right = lax.ppermute(to_left, "band", [(i, (i - 1) % band_count) for i in ring])
    from_left = lax.ppermute(to_right, "band", [(i, (i + 1) % band_count) for i in ring])
    qkv, *own_heads, bias_halo, slot_row, wqkv = call(
        functools.partial(middle_kernel, band_width, experts, capacity),
        [
            shape_of(rows, 3 * width),
            shape_of(rows, width, dtype=F32),
            shape_of(rows, width, dtype=F32),
            shape_of(rows, width, dtype=F32),
            shape_of(tiles, strip, wide_halo, dtype=F32),
            shape_of(8, rows, dtype=I32),
            shape_of(width, 3 * width),
        ],
        [
            info,
            second,
            route_row,
            table_shifted.T,
            qkv_shifted,
        ],
        "savhh",
        [
            pltpu.VMEM(table_shifted.shape[::-1], F32),
            pltpu.VMEM((rows, width), BF),
            pltpu.SemaphoreType.DMA((3,)),
            pltpu.VMEM((HEADS, 2 * LANES), F32),
            pltpu.VMEM((tiles, strip, wide), F32),
        ],
        limit=46.5,
        flops=2 * rows * width * 3 * width,
    )
    from_left, from_right, bias_halo, in_next, out_next = lax.optimization_barrier(
        (from_left, from_right, bias_halo, in_next, out_next)
    )
    in_own, out_own = call(
        stack_kernel,
        [shape_of(2, *expert_in.shape[1:]), shape_of(2, *expert_out.shape[1:])],
        [expert_in[0], in_next, expert_out[0], out_next],
        "vvvv",
        [pltpu.SemaphoreType.DMA((4,))],
        limit=8,
    )
    in_far = swap(in_own, "band", 2)
    out_far = swap(out_own, "band", 1)
    third, *outgoing = call(
        functools.partial(shifted_kernel, band_width, capacity),
        [shape_of(rows, width)] + [shape_of(capacity, width)] * experts,
        [
            info,
            qkv,
            second,
            from_left,
            from_right,
            wqkv,
            *own_heads,
            bias_halo,
            slot_row,
            proj_shifted,
            gain_shifted.reshape(1, width),
        ],
        "svavvvvvvvvhh",
        [
            pltpu.VMEM((2 * sent, 2 * width), BF),
            pltpu.VMEM((rows, width), BF),
            pltpu.VMEM((width, width), BF),
            pltpu.VMEM((1, width), F32),
            pltpu.VMEM((rows, width), BF),
            pltpu.SemaphoreType.DMA((3,)),
        ],
        flops=2 * rows * width * 4 * width,
    )
    weights = [in_own, in_far, out_own, out_far]

    def send(blocks, first):
        return [swap(block, "expert", first + k) for k, block in enumerate(blocks)]

    def compute(blocks):
        return call(
            functools.partial(expert_kernel, len(blocks)),
            [shape_of(capacity, width)] * len(blocks),
            blocks + weights,
            "v" * (len(blocks) + 4),
            flops=4 * len(blocks) * capacity * width * hidden,
        )

    far, most = experts // 2, 3 * experts // 4
    third_part = send(outgoing[far:most], far)
    slot_row, *third_part = lax.optimization_barrier(
        (slot_row, *third_part, *outgoing[most:])
    )
    slot_col = call(column_kernel, [shape_of(rows, LANES, dtype=I32)], [slot_row], "v")[0]
    fourth_part = send(third_part[most - far :], most)
    third_part = compute(third_part[: most - far])
    *third_part, = lax.optimization_barrier((*third_part, *outgoing[:far]))
    near = third_part[most - far :]
    near = near[:1] + send(near[1:], 1)
    back_third = send(third_part[: most - far], far)
    back_fourth = send(compute(fourth_part), most)
    half = far // 2
    first_part, second_part = compute(near[:half]), compute(near[half:])
    returned = (
        first_part[:1]
        + send(first_part[1:], 1)
        + send(second_part, half)
        + back_third
        + back_fourth
    )
    encoded = call(
        functools.partial(final_kernel, band_width, capacity),
        [shape_of(rows, width)],
        [third, slot_col, gain_expert.reshape(1, width)] + returned,
        "vvh" + "v" * experts,
        [pltpu.VMEM((1, width), F32), pltpu.SemaphoreType.DMA((1,))],
        flops=2 * rows * width * 2 * rows,
    )[0]
    return encoded.reshape(crop_count, height, band_width, width)


def solution(mesh):
    return jax.shard_map(
        local,
        mesh=mesh,
        in_specs=(
            P("expert", None, "band", None),
            P("expert", "band", None, None, None),
        )
        + (P(),) * 11
        + (
            P("expert", None, "band"),
            P("expert", "band", None),
            P(),
        ),
        out_specs=P("expert", None, "band", None),
        check_vma=False,
    )
```
